256 devices in a mesh: blk: 64 (over y, x, z_lo, core), grp: 4 (over z_hi).
Axes of the slice: x: 4, y: 4, z: 8 (z_hi: 4, z_lo: 2; z = z_hi * 2 + z_lo), core: 2. Of those that a mesh axis runs over, the one named last changes fastest.
Arguments:
- source_rows: bfloat16 [262144, 400], P(('blk', 'grp')), may hold values from -0.8984375 to 0.8984375
- source_state: float32 [262144], P(('blk', 'grp')), may hold values from 0.002 to 0.02
- target_rows: bfloat16 [262144, 400], P(('blk', 'grp')), may hold values from -0.8984375 to 0.8984375
- target_state: float32 [262144], P(('blk', 'grp')), may hold values from 0.002 to 0.02
- relations: float32 [1024, 400], replicated, may hold values from -6 to 6
- relation_state: float32 [1024], replicated, may hold values from 0.01 to 0.1
- source_ids: int32 [524288], P(('blk', 'grp')), may hold values from 0 to 1023
- relation_ids: int32 [524288], P(('blk', 'grp')), may hold values from 0 to 1023
- target_ids: int32 [524288], P(('blk', 'grp')), may hold values from 0 to 1023
- source_negs: int32 [4096, 1024], P(('blk', 'grp')), may hold values from 0 to 1023
- target_negs: int32 [4096, 1024], P(('blk', 'grp')), may hold values from 0 to 1023
- edge_counts: int32 [256], P(('blk', 'grp')), may hold values from 256 to 2048, as said below
Outputs:
- source_out: bfloat16 [262144, 400], P(('blk', 'grp'))
- source_state_out: float32 [262144], P(('blk', 'grp'))
- target_out: bfloat16 [262144, 400], P(('blk', 'grp'))
- target_state_out: float32 [262144], P(('blk', 'grp'))
- relations_out: float32 [1024, 400], replicated
- relation_state_out: float32 [1024], replicated
The draws below stay inside these ranges and needn't reach their ends.
Inputs may be any that keep to these rules, and one draw needn't show every extreme that they name: `edge_counts`: each bucket's count is 2048, 1024, 512 or 256, so whole blocks are live; in every draw some bucket has 2048.
All inputs are finite; a program needn't handle non-finite values.
Results may differ from the reference program's by a relative error of at most 0.0016.
Values may be sent and summed in bfloat16 or wider, within the bound.
A program may use at most 64 MiB of HBM per device.

```python
import math
import jax
import jax.numpy as jnp
from jax import lax

W = 400
P_SIZE = 1024
EDGES = 2048
BLOCK = 128
NEG = 1024
R = 1024
BLOCKS = 16
DEVS = 256
ALL_ROWS = 262144
ALL_EDGES = 524288
ALL_BLOCKS = 4096
N_BLK = 64
N_GRP = 4


def draw_edge_counts(key, part):
    halvings = jax.random.randint(key, (DEVS,), 0, 4)
    counts = EDGES // jnp.power(2, halvings)
    chosen = jax.random.randint(jax.random.fold_in(key, 7), (), 0, DEVS)
    counts = counts.at[chosen].set(EDGES)
    return counts.astype(jnp.int32)


def draw_relation_ids(key, part):
    own_span = R // DEVS
    bucket = jnp.arange(ALL_EDGES, dtype=jnp.int32) // EDGES
    own_pick = bucket * own_span + jax.random.randint(jax.random.fold_in(key, 11), (ALL_EDGES,), 0, own_span)
    shared_pick = jax.random.randint(jax.random.fold_in(key, 13), (ALL_EDGES,), 0, R)
    selector = jax.random.randint(jax.random.fold_in(key, 17), (ALL_EDGES,), 0, 10)
    return jnp.where(selector < 9, own_pick, shared_pick).astype(jnp.int32)


def set_ends(drawn, key, smallest, largest):
    dims = drawn.shape
    index_at = [jax.random.randint(jax.random.fold_in(key, axis), (), 0, dims[axis]) for axis in range(len(dims))]
    drawn = drawn.at[tuple(index_at)].set(smallest)
    longest = dims.index(max(dims))
    index_at[longest] = (index_at[longest] + 1) % dims[longest]
    return drawn.at[tuple(index_at)].set(largest)


def level_of(stream_key, dims, split, least, largest):
    factor_of, own = 1.0, jax.random.fold_in(stream_key, 6)
    for axis_at, parts in split:
        heights = jnp.exp(jax.random.uniform(jax.random.fold_in(own, axis_at), (parts,), jnp.float32, least / len(split), largest / len(split)))
        factor_of = factor_of * jnp.repeat(heights, dims[axis_at] // parts).reshape([-1 if axis == axis_at else 1 for axis in range(len(dims))])
    return factor_of


def centred(stream_key, dims, scale, reach, cuts=(), held_as=jnp.bfloat16):
    result = scale * jax.random.normal(stream_key, dims, jnp.float32)
    if cuts:
        result = result * level_of(stream_key, dims, cuts, -0.22, 0.18)
    return jnp.clip(result, -reach, reach).astype(held_as)


def setup_inputs(seed: int = 0) -> dict:
    keys = jax.random.split(jax.random.key(seed), 13)
    return {
        "source_rows": centred(keys[0], (ALL_ROWS, W), 0.15, 0.8984375, ((0, 256),)),
        "source_state": jnp.clip(jnp.exp(math.log(0.02) - 2.30258502 * jax.random.uniform(keys[1], (ALL_ROWS,), jnp.float32) ** level_of(keys[1], (ALL_ROWS,), ((0, 256),), -0.2, 0.2)), 0.002, 0.02),
        "target_rows": centred(keys[2], (ALL_ROWS, W), 0.15, 0.8984375, ((0, 256),)),
        "target_state": jnp.clip(jnp.exp(math.log(0.02) - 2.30258502 * jax.random.uniform(keys[3], (ALL_ROWS,), jnp.float32) ** level_of(keys[3], (ALL_ROWS,), ((0, 256),), -0.2, 0.2)), 0.002, 0.02),
        "relations": centred(keys[4], (R, W), 1.0, 6.0, (), jnp.float32),
        "relation_state": jnp.clip(jnp.exp(jax.random.uniform(keys[5], (R,), jnp.float32, math.log(0.01), math.log(0.1))), 0.01, 0.1),
        "source_ids": set_ends(jax.random.randint(keys[6], (ALL_EDGES,), 0, P_SIZE), jax.random.fold_in(keys[6], 1), 0, P_SIZE - 1).astype(jnp.int32),
        "relation_ids": draw_relation_ids(jax.random.fold_in(keys[12], 71), 0),
        "target_ids": set_ends(jax.random.randint(keys[8], (ALL_EDGES,), 0, P_SIZE), jax.random.fold_in(keys[8], 1), 0, P_SIZE - 1).astype(jnp.int32),
        "source_negs": set_ends(jax.random.randint(keys[9], (ALL_BLOCKS, NEG), 0, P_SIZE), jax.random.fold_in(keys[9], 1), 0, P_SIZE - 1).astype(jnp.int32),
        "target_negs": set_ends(jax.random.randint(keys[10], (ALL_BLOCKS, NEG), 0, P_SIZE), jax.random.fold_in(keys[10], 1), 0, P_SIZE - 1).astype(jnp.int32),
        "edge_counts": draw_edge_counts(jax.random.fold_in(keys[12], 71), 0),
    }


learn_rate = 0.1

def split_halves(values):
    middle = values.shape[-1] // 2
    return (values[..., :middle], values[..., middle:])

def complex_product(left, right):
    left_re, left_im = split_halves(left)
    right_re, right_im = split_halves(right)
    return jnp.concatenate([left_re * right_re - left_im * right_im, left_re * right_im + left_im * right_re], axis=-1)

def conj_product(left, right):
    left_re, left_im = split_halves(left)
    right_re, right_im = split_halves(right)
    return jnp.concatenate([left_re * right_re + left_im * right_im, left_im * right_re - left_re * right_im], axis=-1)

def block_step(block, carry, tables):
    source_rows, target_rows, relations, source_ids, relation_ids, target_ids, source_negs, target_negs = tables
    source_grad, target_grad, relation_grad = carry
    first = (block * BLOCK).astype(jnp.int32)
    pick_source = lax.dynamic_slice_in_dim(source_ids, first, BLOCK)
    pick_relation = lax.dynamic_slice_in_dim(relation_ids, first, BLOCK)
    pick_target = lax.dynamic_slice_in_dim(target_ids, first, BLOCK)
    source_vec = jnp.take(source_rows, pick_source, axis=0).astype(jnp.float32)
    target_vec = jnp.take(target_rows, pick_target, axis=0).astype(jnp.float32)
    relation_vec = jnp.take(relations, pick_relation, axis=0)
    query = complex_product(source_vec, relation_vec)
    probe = conj_product(relation_vec, target_vec)
    positive = lax.optimization_barrier(jnp.sum(query * target_vec, axis=-1))
    query_low = query.astype(jnp.bfloat16)
    probe_low = probe.astype(jnp.bfloat16)
    neg_target_ids = target_negs[block]
    neg_source_ids = source_negs[block]
    neg_target = jnp.take(target_rows, neg_target_ids, axis=0)
    neg_source = jnp.take(source_rows, neg_source_ids, axis=0)
    contract_last = (((1,), (1,)), ((), ()))
    contract_first = (((0,), (0,)), ((), ()))
    target_scores = lax.dot_general(query_low, neg_target, contract_last, preferred_element_type=jnp.float32)
    source_scores = lax.dot_general(probe_low, neg_source, contract_last, preferred_element_type=jnp.float32)
    pos_grad = -jax.nn.sigmoid(-positive)
    neg_count = target_scores.shape[1]
    target_weight = (jax.nn.sigmoid(target_scores) / neg_count).astype(jnp.bfloat16)
    source_weight = (jax.nn.sigmoid(source_scores) / neg_count).astype(jnp.bfloat16)
    query_grad = pos_grad[:, None] * target_vec + jnp.dot(target_weight, neg_target, preferred_element_type=jnp.float32)
    probe_grad = jnp.dot(source_weight, neg_source, preferred_element_type=jnp.float32)
    neg_target_grad = lax.dot_general(target_weight, query_low, contract_first, preferred_element_type=jnp.float32)
    neg_source_grad = lax.dot_general(source_weight, probe_low, contract_first, preferred_element_type=jnp.float32)
    source_grad = source_grad.at[pick_source].add(conj_product(query_grad, relation_vec))
    source_grad = source_grad.at[neg_source_ids].add(neg_source_grad)
    target_grad = target_grad.at[pick_target].add(pos_grad[:, None] * query + complex_product(probe_grad, relation_vec))
    target_grad = target_grad.at[neg_target_ids].add(neg_target_grad)
    relation_term = conj_product(query_grad, source_vec) + conj_product(target_vec, probe_grad)
    relation_grad = relation_grad.at[pick_relation].add(relation_term)
    return (source_grad, target_grad, relation_grad)

def adagrad(params, state, grad):
    new_state = state + lax.optimization_barrier(jnp.mean(grad * grad, axis=1))
    new_params = params.astype(jnp.float32) - learn_rate * grad / jnp.sqrt(new_state)[:, None]
    return (new_params, new_state)

def reference(source_rows, source_state, target_rows, target_state, relations, relation_state, source_ids, relation_ids, target_ids, source_negs, target_negs, edge_counts):
    stacked = (source_rows.reshape(DEVS, P_SIZE, W), source_state.reshape(DEVS, P_SIZE), target_rows.reshape(DEVS, P_SIZE, W), target_state.reshape(DEVS, P_SIZE), source_ids.reshape(DEVS, EDGES), relation_ids.reshape(DEVS, EDGES), target_ids.reshape(DEVS, EDGES), source_negs.reshape(DEVS, BLOCKS, NEG), target_negs.reshape(DEVS, BLOCKS, NEG), edge_counts)

    def per_bucket(total, pieces):
        src_rows, src_state, tgt_rows, tgt_state, src_ids, rel_ids, tgt_ids, src_negs, tgt_negs, live_count = pieces
        tables = (src_rows, tgt_rows, relations, src_ids, rel_ids, tgt_ids, src_negs, tgt_negs)
        start = (jnp.zeros((P_SIZE, W), jnp.float32), jnp.zeros((P_SIZE, W), jnp.float32), jnp.zeros((R, W), jnp.float32))
        source_grad, target_grad, relation_grad = lax.fori_loop(jnp.int32(0), (live_count // BLOCK).astype(jnp.int32), lambda block, carry: block_step(block, carry, tables), start)
        new_source, new_source_state = adagrad(src_rows, src_state, source_grad)
        new_target, new_target_state = adagrad(tgt_rows, tgt_state, target_grad)
        return (total + relation_grad, (new_source.astype(jnp.bfloat16), new_source_state, new_target.astype(jnp.bfloat16), new_target_state))
    total, results = lax.scan(per_bucket, jnp.zeros((R, W), jnp.float32), stacked)
    new_source, new_source_state, new_target, new_target_state = results
    half_axis = N_BLK // 2
    moved_target = jnp.roll(new_target.reshape(N_BLK, N_GRP, P_SIZE, W), half_axis, axis=0)
    moved_state = jnp.roll(new_target_state.reshape(N_BLK, N_GRP, P_SIZE), half_axis, axis=0)
    relations_out, relation_state_out = adagrad(relations, relation_state, total)
    return (new_source.reshape(ALL_ROWS, W), new_source_state.reshape(ALL_ROWS), moved_target.reshape(ALL_ROWS, W), moved_state.reshape(ALL_ROWS), relations_out, relation_state_out)
```

```python
import jax
import jax.numpy as jnp
from jax import lax
from jax.experimental import pallas as pl
from jax.experimental.pallas import tpu as pltpu
from jax.sharding import PartitionSpec as P

F32, BF16 = jnp.float32, jnp.bfloat16
W, HALF, ROWS, EDGES, BLOCK, NEG = 400, 200, 1024, 2048, 128, 1024
CHUNK = 256
PART = 208
RATE = 0.1
NN = (((1,), (0,)), ((), ()))
NT = (((1,), (1,)), ((), ()))
MESH = pl.DeviceIdType.MESH
SIZE = {"y": 4, "x": 4, "z": 8, "core": 2}
HOPS = {"y": (1, 3, 2), "x": (1, 3, 2), "z": (4, 3, 5, 2, 6, 1, 7), "core": (1,)}


def place():
    blk, grp = lax.axis_index("blk"), lax.axis_index("grp")
    return {"y": blk // 16, "x": blk // 4 % 4, "z": grp * 2 + blk // 2 % 2, "core": blk % 2}


def peer(me, axis, hop):
    at = dict(me)
    at[axis] = lax.rem(me[axis] + hop, SIZE[axis])
    return (at["y"] * 16 + at["x"] * 4 + at["z"] % 2 * 2 + at["core"], at["z"] // 2)


def dot(a, b, dims=NN):
    return lax.dot_general(a, b, dims, preferred_element_type=F32)


def mul(a, b):
    ar, ai, br, bi = a[:HALF], a[HALF:], b[:HALF], b[HALF:]
    return jnp.concatenate([ar * br - ai * bi, ar * bi + ai * br], axis=0)


def mulc(a, b):
    ar, ai, br, bi = a[:HALF], a[HALF:], b[:HALF], b[HALF:]
    return jnp.concatenate([ar * br + ai * bi, ai * br - ar * bi], axis=0)


def split(x):
    hi = x.astype(BF16)
    return hi, (x - hi.astype(F32)).astype(BF16)


def one_hot(ids, count):
    at = lax.broadcasted_iota(jnp.int32, (count, ids.shape[1]), 0)
    return jnp.where(at == ids, 1.0, 0.0).astype(BF16)


def counts_of(ids, scale):
    grid = dot(one_hot(ids % 32, 32), one_hot(ids // 32, 32), NT) * scale
    return jnp.concatenate([jnp.broadcast_to(grid[:, h : h + 1], (32, BLOCK)) for h in range(32)], axis=0)


def weights_of(scores, count):
    return (count + count * jnp.tanh(scores)).astype(BF16)


def update(table, state, grad):
    new_state = state + jnp.sum(grad * grad, axis=0, keepdims=True) * (1.0 / W)
    return table - RATE * grad * lax.rsqrt(new_state), new_state


def aligned(index, size):
    return pl.ds(pl.multiple_of(index * size, size), size)


def bucket_kernel(
    live_ref, src_ref, src_state, tgt_ref, tgt_state, rel_ref, sid_ref, rid_ref, did_ref, sneg_ref, tneg_ref,
    src_out, src_state_out, tgt_out, tgt_state_out, rel_sum,
    src_t, tgt_t, rel_hl, oh_s, oh_d, oh_r, w_s, w_t, q_low, p_low, gs_hi, gs_lo, gt_hi, gt_lo, rt,
    tgt_new, tgt_state_new, own, other, from_x, at_z, from_z, at_y, from_y, got_y, got_x, got_core,
    core_s, core_r, x_s, x_r, z_s, z_r, y_s, y_r, gy_s, gy_r, gz_s, gz_r, gx_s, gx_r, gc_s, gc_r,
    t_s, t_r, ts_s, ts_r, out_sem,
):
    me = place()
    core, x, y, z = me["core"], me["x"], me["y"], me["z"]
    barrier = pltpu.get_barrier_semaphore()
    total = 0
    for axis, hops in HOPS.items():
        for hop in hops:
            pl.semaphore_signal(barrier, inc=1, device_id=peer(me, axis, hop), device_id_type=MESH)
            total += 1

    def send(src, dst, send_sem, recv_sem, axis, hop):
        return pltpu.make_async_remote_copy(
            src_ref=src, dst_ref=dst, send_sem=send_sem, recv_sem=recv_sem,
            device_id=peer(me, axis, hop), device_id_type=MESH,
        )

    src_t[...] = (0.5 * src_ref[...].astype(F32)).T.astype(BF16)
    tgt_t[...] = (0.5 * tgt_ref[...].astype(F32)).T.astype(BF16)
    hi, lo = split(rel_ref[...])
    rel_hl[:W] = hi
    rel_hl[W:] = lo
    own[:, W:] = jnp.zeros((8, 2 * PART - W, 128), BF16)
    at_z[:, PART:] = jnp.zeros((2, 256 - PART, 128), BF16)
    count = live_ref[0]

    def edges(c, _):
        first = pl.multiple_of(c * CHUNK, CHUNK)
        here = pl.ds(first, CHUNK)
        scale = jnp.where(first < count, 0.5 / NEG, 0.0).astype(F32)
        alive = jnp.where(first < count, 1.0, 0.0).astype(F32)
        ohs = one_hot(sid_ref[:, here], ROWS)
        ohd = one_hot(did_ref[:, here], ROWS)
        ohr = one_hot(rid_ref[:, here], ROWS)
        oh_s[:, here] = ohs
        oh_d[:, here] = ohd
        oh_r[:, here] = ohr
        s = dot(src_ref[...], ohs)
        d = dot(tgt_ref[...], ohd)
        both = dot(rel_hl[...], ohr)
        r = both[:W] + both[W:]
        q = mul(s, r)
        p = mulc(r, d)
        pos = jnp.sum(q * d, axis=0, keepdims=True)
        pos_grad = -alive / (1.0 + jnp.exp(pos))
        ql = q.astype(BF16)
        plow = p.astype(BF16)
        q_low[:, here] = ql
        p_low[:, here] = plow
        ct = jnp.concatenate([counts_of(tneg_ref[pl.ds(2 * c + i, 1), :], scale) for i in range(2)], axis=1)
        wt = weights_of(dot(tgt_t[...], ql), ct)
        w_t[:, here] = wt
        cs = jnp.concatenate([counts_of(sneg_ref[pl.ds(2 * c + i, 1), :], scale) for i in range(2)], axis=1)
        ws = weights_of(dot(src_t[...], plow), cs)
        w_s[:, here] = ws
        qg = pos_grad * d + dot(tgt_ref[...], wt)
        pg = dot(src_ref[...], ws)
        gs_hi[:, here], gs_lo[:, here] = split(mulc(qg, r))
        gt_hi[:, here], gt_lo[:, here] = split(pos_grad * q + mul(pg, r))
        rt[:, here] = (mulc(qg, s) + mulc(d, pg)).astype(BF16)
        return 0

    lax.fori_loop(0, EDGES // CHUNK, edges, 0)
    pl.semaphore_wait(barrier, total)

    half = aligned(core, PART)
    far = aligned(1 - core, PART)
    order = HOPS["x"] + (0,)

    def piece(i):
        return lax.rem(x + order[i], 4)

    def core_copy(i):
        tiles = pl.ds(2 * piece(i), 2)
        return send(own.at[tiles, far], other.at[tiles], core_s.at[i], core_r.at[i], "core", 1)

    def x_copy(i):
        return send(other.at[pl.ds(2 * piece(i), 2)], from_x.at[i], x_s.at[i], x_r.at[i], "x", order[i])

    def relation_piece(i):
        j = piece(i)
        grad = dot(rt[...], oh_r[aligned(j, CHUNK), :], NT).astype(BF16)
        own[2 * j, :W] = grad[:, :128]
        own[2 * j + 1, :W] = grad[:, 128:]
        core_copy(i).start()

    def core_add(i):
        core_copy(i).wait_recv()
        tiles = pl.ds(2 * piece(i), 2)
        other[tiles] = (other[tiles].astype(F32) + own[tiles, half].astype(F32)).astype(BF16)

    for i in range(4):
        relation_piece(i)
        if i:
            core_add(i - 1)
            x_copy(i - 1).start()
    core_add(3)

    def rows_step(c, table, state, hi_ref, lo_ref, oh, low, wts):
        here = aligned(c, CHUNK)
        grad = dot(hi_ref[...], oh[here, :], NT) + dot(lo_ref[...], oh[here, :], NT) + dot(low[...], wts[here, :], NT)
        return here, update(table[:, here].astype(F32), state[:, here], grad)

    def target_copy(c):
        here = aligned(c, CHUNK)
        return send(tgt_new.at[:, here], tgt_out.at[:, here], t_s.at[c], t_r.at[c], "y", 2)

    def target_step(c, _):
        here, (new, new_state) = rows_step(c, tgt_ref, tgt_state, gt_hi, gt_lo, oh_d, q_low, w_t)
        tgt_new[:, here] = new.astype(BF16)
        tgt_state_new[:, here] = new_state
        target_copy(c).start()
        return 0

    def source_step(c, _):
        here, (new, new_state) = rows_step(c, src_ref, src_state, gs_hi, gs_lo, oh_s, p_low, w_s)
        src_out[:, here] = new.astype(BF16)
        src_state_out[:, here] = new_state
        return 0

    lax.fori_loop(0, 3, target_step, 0)
    for i in range(3):
        x_copy(i).wait_recv()
    mine = pl.ds(2 * x, 2)
    at_z[:, :PART] = (
        other[mine].astype(F32) + from_x[0].astype(F32) + from_x[1].astype(F32) + from_x[2].astype(F32)
    ).astype(BF16)
    z_hops, y_hops = HOPS["z"], HOPS["y"]
    z_copies = []
    for i, hop in enumerate(z_hops):
        to = lax.rem(z + hop, 8)
        z_copies.append(send(at_z.at[to // 4, aligned(to % 4, 64)], from_z.at[i], z_s.at[i], z_r.at[i], "z", hop))
        z_copies[-1].start()
    lax.fori_loop(3, 4, target_step, 0)
    state_copy = send(tgt_state_new, tgt_state_out, ts_s, ts_r, "y", 2)
    state_copy.start()
    for copy in z_copies:
        copy.wait_recv()
    summed = at_z[z // 4, aligned(z % 4, 64), :].astype(F32)
    for i in range(7):
        summed = summed + from_z[i].astype(F32)
    at_y[...] = summed.astype(BF16)
    y_copies = []
    for i, hop in enumerate(y_hops):
        to = lax.rem(y + hop, 4)
        y_copies.append(send(at_y.at[aligned(to, 16)], from_y.at[i], y_s.at[i], y_r.at[i], "y", hop))
        y_copies[-1].start()
    lax.fori_loop(0, 1, source_step, 0)
    for copy in y_copies:
        copy.wait_recv()
    tile = aligned(y, 16)
    summed = at_y[tile, :].astype(F32)
    for i in range(3):
        summed = summed + from_y[i].astype(F32)
    got_y[tile, :] = summed.astype(BF16)
    back_y = []
    for i, hop in enumerate(y_hops):
        back_y.append(send(got_y.at[tile], got_y.at[tile], gy_s.at[i], gy_r.at[i], "y", hop))
        back_y[-1].start()
    lax.fori_loop(1, 2, source_step, 0)
    for copy in back_y:
        copy.wait_recv()
    slot = got_x.at[x, z // 4, aligned(z % 4, 64)]
    back_z = []
    for i, hop in enumerate(z_hops):
        back_z.append(send(got_y, slot, gz_s.at[i], gz_r.at[i], "z", hop))
        back_z[-1].start()
    got_x[x, z // 4, aligned(z % 4, 64), :] = got_y[...]
    lax.fori_loop(2, 3, source_step, 0)
    for copy in back_z:
        copy.wait_recv()
    back_x = []
    for i, hop in enumerate(HOPS["x"]):
        ready = got_x.at[x, :, pl.ds(0, PART)]
        back_x.append(send(ready, ready, gx_s.at[i], gx_r.at[i], "x", hop))
        back_x[-1].start()

    def to_core(i, index):
        return send(got_x.at[index, :, pl.ds(0, PART)], got_core.at[index], gc_s.at[i], gc_r.at[i], "core", 1)

    cores = [to_core(0, x)]
    cores[0].start()
    lax.fori_loop(3, 4, source_step, 0)
    for i, hop in enumerate(HOPS["x"]):
        back_x[i].wait_recv()
        cores.append(to_core(i + 1, lax.rem(x + 4 - hop, 4)))
        cores[-1].start()
    out_own = pltpu.make_async_copy(got_x.at[:, :, pl.ds(0, PART)], rel_sum.at[core], out_sem.at[0])
    out_own.start()
    for copy in cores:
        copy.wait_recv()
    out_far = pltpu.make_async_copy(got_core, rel_sum.at[1 - core], out_sem.at[1])
    out_far.start()
    for i in range(4):
        core_copy(i).wait_send()
        target_copy(i).wait()
    for i in range(3):
        x_copy(i).wait_send()
    for copy in z_copies + y_copies + back_y + back_z + back_x + cores:
        copy.wait_send()
    state_copy.wait()
    out_own.wait()
    out_far.wait()


def finish_kernel(src, src_state, tgt, tgt_state, sums, rel, rel_state,
                  src_out, src_state_out, tgt_out, tgt_state_out, rel_out, rel_state_out, sem):
    copies = [
        pltpu.make_async_copy(a, b, sem.at[i])
        for i, (a, b) in enumerate(
            [(src, src_out), (tgt, tgt_out), (src_state, src_state_out), (tgt_state, tgt_state_out)]
        )
    ]
    for copy in copies:
        copy.start()
    for t in range(8):
        here = slice(128 * t, 128 * t + 128)
        grad = jnp.concatenate([sums[0, t // 2, t % 2], sums[1, t // 2, t % 2, : W - PART]], axis=0).astype(F32)
        new, new_state = update(rel[:, here], rel_state[:, here], grad)
        rel_out[:, here] = new
        rel_state_out[:, here] = new_state
    for copy in copies:
        copy.wait()


def shards(src, src_state, tgt, tgt_state, rel, rel_state, sid, rid, did, sneg, tneg, live):
    vm = pl.BlockSpec(memory_space=pltpu.VMEM)
    sm = pl.BlockSpec(memory_space=pltpu.SMEM)
    hbm = pl.BlockSpec(memory_space=pl.ANY)
    shape = jax.ShapeDtypeStruct
    dma = pltpu.SemaphoreType.DMA

    def vmem(*dims, dtype=BF16):
        return pltpu.VMEM(dims, dtype)

    rows_bf, row_f = shape((W, ROWS), BF16), shape((1, ROWS), F32)
    wide = [(1, ROWS), (1, EDGES)]
    new_src, new_src_state, new_tgt, new_tgt_state, sums = pl.pallas_call(
        bucket_kernel,
        out_shape=(rows_bf, row_f, rows_bf, row_f, shape((2, 4, 2, PART, 128), BF16)),
        in_specs=[sm] + [vm] * 10,
        out_specs=[vm, vm, hbm, hbm, hbm],
        scratch_shapes=[vmem(ROWS, W), vmem(ROWS, W), vmem(2 * W, ROWS)]
        + [vmem(ROWS, EDGES)] * 5
        + [vmem(W, EDGES)] * 7
        + [
            vmem(W, ROWS), vmem(1, ROWS, dtype=F32), vmem(8, 2 * PART, 128), vmem(8, PART, 128),
            vmem(3, 2, PART, 128), vmem(2, 256, 128), vmem(7, 64, 128), vmem(64, 128), vmem(3, 16, 128),
            vmem(64, 128), vmem(4, 2, 256, 128), vmem(4, 2, PART, 128),
        ]
        + [dma((n,)) for n in (4, 4, 3, 3, 7, 7, 3, 3, 3, 3, 7, 7, 3, 3, 4, 4, 4, 4)]
        + [dma(()), dma(()), dma((2,))],
        compiler_params=pltpu.CompilerParams(
            collective_id=0, has_side_effects=True, vmem_limit_bytes=60 * 2**20
        ),
        name="bucket",
    )(live, src.T, src_state.reshape(wide[0]), tgt.T, tgt_state.reshape(wide[0]), rel.T,
      sid.reshape(wide[1]), rid.reshape(wide[1]), did.reshape(wide[1]), sneg, tneg)
    outs = pl.pallas_call(
        finish_kernel,
        out_shape=(rows_bf, row_f, rows_bf, row_f, shape((W, ROWS), F32), row_f),
        in_specs=[vm] * 7,
        out_specs=[hbm] * 4 + [vm] * 2,
        scratch_shapes=[dma((4,))],
        name="finish",
    )(new_src, new_src_state, new_tgt, new_tgt_state, sums, rel.T, rel_state.reshape(wide[0]))
    return (outs[0].T, outs[1].reshape(ROWS), outs[2].T, outs[3].reshape(ROWS), outs[4].T, outs[5].reshape(ROWS))


def solution(mesh):
    split_rows, split_one, copied = P(("blk", "grp"), None), P(("blk", "grp")), P()
    return jax.shard_map(
        shards,
        mesh=mesh,
        in_specs=(split_rows, split_one, split_rows, split_one, copied, copied,
                  split_one, split_one, split_one, split_rows, split_rows, split_one),
        out_specs=(split_rows, split_one, split_rows, split_one, copied, copied),
        check_vma=False,
    )
```

```python
import jax
import jax.numpy as jnp
from jax import lax
from jax.experimental import pallas as pl
from jax.experimental.pallas import tpu as pltpu
from jax.sharding import PartitionSpec as P

F32, BF16 = jnp.float32, jnp.bfloat16
W, HALF, ROWS, EDGES, BLOCK, NEG = 400, 200, 1024, 2048, 128, 1024
CHUNK = 256
PART = 208
RATE = 0.1
NN = (((1,), (0,)), ((), ()))
NT = (((1,), (1,)), ((), ()))
MESH = pl.DeviceIdType.MESH
SIZE = {"y": 4, "x": 4, "z": 8, "core": 2}
HOPS = {"y": (2, 1, 3), "x": (2, 1, 3), "z": (4, 3, 5, 2, 6, 1, 7), "core": (1,)}


def place():
    blk, grp = lax.axis_index("blk"), lax.axis_index("grp")
    return {"y": blk // 16, "x": blk // 4 % 4, "z": grp * 2 + blk // 2 % 2, "core": blk % 2}


def peer(me, axis, hop):
    at = dict(me)
    at[axis] = lax.rem(me[axis] + hop, SIZE[axis])
    return (at["y"] * 16 + at["x"] * 4 + at["z"] % 2 * 2 + at["core"], at["z"] // 2)


def dot(a, b, dims=NN):
    return lax.dot_general(a, b, dims, preferred_element_type=F32)


def mul(a, b):
    ar, ai, br, bi = a[:HALF], a[HALF:], b[:HALF], b[HALF:]
    return jnp.concatenate([ar * br - ai * bi, ar * bi + ai * br], axis=0)


def mulc(a, b):
    ar, ai, br, bi = a[:HALF], a[HALF:], b[:HALF], b[HALF:]
    return jnp.concatenate([ar * br + ai * bi, ai * br - ar * bi], axis=0)


def split(x):
    hi = x.astype(BF16)
    return hi, (x - hi.astype(F32)).astype(BF16)


def one_hot(ids, count):
    at = lax.broadcasted_iota(jnp.int32, (count, ids.shape[1]), 0)
    return jnp.where(at == ids, 1.0, 0.0).astype(BF16)


def pick(table, ids):
    low, high = ids % 128, ids // 128
    parts = []
    for b in range(ids.shape[1] // 128):
        lanes = slice(128 * b, 128 * b + 128)
        at = jnp.broadcast_to(low[:, lanes], (W, 128))
        tile = jnp.broadcast_to(high[:, lanes], (W, 128))
        out = jnp.take_along_axis(table[:, :128], at, axis=1, mode="promise_in_bounds")
        for t in range(1, ROWS // 128):
            got = jnp.take_along_axis(table[:, 128 * t : 128 * t + 128], at, axis=1, mode="promise_in_bounds")
            out = jnp.where(tile == t, got, out)
        parts.append(out)
    return jnp.concatenate(parts, axis=1)


def counts_of(ids, scale):
    grid = dot(one_hot(ids % 32, 32), one_hot(ids // 32, 32), NT) * scale
    return jnp.concatenate([jnp.broadcast_to(grid[:, h : h + 1], (32, BLOCK)) for h in range(32)], axis=0)


def weights_of(scores, count):
    return (count + count * jnp.tanh(scores)).astype(BF16)


def update(table, state, grad):
    new_state = state + jnp.sum(grad * grad, axis=0, keepdims=True) * (1.0 / W)
    return table - RATE * grad * lax.rsqrt(new_state), new_state


def aligned(index, size):
    return pl.ds(pl.multiple_of(index * size, size), size)


def bucket_kernel(
    live_ref, src_h, src_state_h, tgt_h, tgt_state_h, rel_h, rel_state_h, sid_h, rid_h, did_h, sneg_h, tneg_h,
    src_out, src_state_out, tgt_out, tgt_state_out, rel_out, rel_state_out,
    src_ref, src_state, tgt_ref, tgt_state, rel_ref, rel_state, sid_ref, rid_ref, did_ref, sneg_ref, tneg_ref, in_sem,
    src_t, tgt_t, oh_s, oh_d, oh_r, w_s, w_t, q_low, p_low, gs_hi, gs_lo, gt_hi, gt_lo, rt,
    tgt_new, tgt_state_new, own, other, from_x, at_z, from_z, from_y, got_y, got,
    core_s, core_r, x_s, x_r, z_s, z_r, y_s, y_r, gz_s, gz_r, gx_s, gx_r, gc_s, gc_r,
    t_s, t_r, ts_s, ts_r,
):
    loads = [
        pltpu.make_async_copy(here, there, in_sem.at[i])
        for i, (here, there) in enumerate([
            (src_h, src_ref), (tgt_h, tgt_ref), (rel_h, rel_ref), (sid_h, sid_ref), (rid_h, rid_ref), (did_h, did_ref),
            (sneg_h, sneg_ref), (tneg_h, tneg_ref), (src_state_h, src_state), (tgt_state_h, tgt_state),
            (rel_state_h, rel_state),
        ])
    ]
    for load in loads:
        load.start()
    me = place()
    core, x, y, z = me["core"], me["x"], me["y"], me["z"]
    barrier = pltpu.get_barrier_semaphore()
    total = 0
    for axis, hops in HOPS.items():
        for hop in hops:
            pl.semaphore_signal(barrier, inc=1, device_id=peer(me, axis, hop), device_id_type=MESH)
            total += 1

    def send(src, dst, send_sem, recv_sem, axis, hop):
        return pltpu.make_async_remote_copy(
            src_ref=src, dst_ref=dst, send_sem=send_sem, recv_sem=recv_sem,
            device_id=peer(me, axis, hop), device_id_type=MESH,
        )

    own[:, W:] = jnp.zeros((8, 2 * PART - W, 128), BF16)
    at_z[:, PART:] = jnp.zeros((2, 256 - PART, 128), BF16)
    loads[0].wait()
    src_t[...] = (0.5 * src_ref[...].astype(F32)).T.astype(BF16)
    loads[1].wait()
    tgt_t[...] = (0.5 * tgt_ref[...].astype(F32)).T.astype(BF16)
    for load in loads[2:]:
        load.wait()
    count = live_ref[0]

    def edges(c, _):
        first = pl.multiple_of(c * CHUNK, CHUNK)
        here = pl.ds(first, CHUNK)
        scale = jnp.where(first < count, 0.5 / NEG, 0.0).astype(F32)
        alive = jnp.where(first < count, 1.0, 0.0).astype(F32)
        ohs = one_hot(sid_ref[:, here], ROWS)
        ohd = one_hot(did_ref[:, here], ROWS)
        ohr = one_hot(rid_ref[:, here], ROWS)
        oh_s[:, here] = ohs
        oh_d[:, here] = ohd
        oh_r[:, here] = ohr
        s = dot(src_ref[...], ohs)
        d = dot(tgt_ref[...], ohd)
        r = pick(rel_ref, rid_ref[:, here])
        q = mul(s, r)
        p = mulc(r, d)
        pos = jnp.sum(q * d, axis=0, keepdims=True)
        pos_grad = -alive / (1.0 + jnp.exp(pos))
        ql = q.astype(BF16)
        plow = p.astype(BF16)
        q_low[:, here] = ql
        p_low[:, here] = plow
        ct = jnp.concatenate([counts_of(tneg_ref[pl.ds(2 * c + i, 1), :], scale) for i in range(2)], axis=1)
        wt = weights_of(dot(tgt_t[...], ql), ct)
        w_t[:, here] = wt
        cs = jnp.concatenate([counts_of(sneg_ref[pl.ds(2 * c + i, 1), :], scale) for i in range(2)], axis=1)
        ws = weights_of(dot(src_t[...], plow), cs)
        w_s[:, here] = ws
        qg = pos_grad * d + dot(tgt_ref[...], wt)
        pg = dot(src_ref[...], ws)
        gs_hi[:, here], gs_lo[:, here] = split(mulc(qg, r))
        gt_hi[:, here], gt_lo[:, here] = split(pos_grad * q + mul(pg, r))
        rt[:, here] = (mulc(qg, s) + mulc(d, pg)).astype(BF16)
        return 0

    lax.fori_loop(0, EDGES // CHUNK, edges, 0)
    pl.semaphore_wait(barrier, total)

    half = aligned(core, PART)
    far = aligned(1 - core, PART)
    order = HOPS["x"] + (0,)

    def piece(i):
        return lax.rem(x + order[i], 4)

    def core_copy(i):
        tiles = pl.ds(2 * piece(i), 2)
        return send(own.at[tiles, far], other.at[tiles], core_s.at[i], core_r.at[i], "core", 1)

    def x_copy(i):
        return send(other.at[pl.ds(2 * piece(i), 2)], from_x.at[i], x_s.at[i], x_r.at[i], "x", order[i])

    def relation_piece(i):
        j = piece(i)
        grad = dot(rt[...], oh_r[aligned(j, CHUNK), :], NT).astype(BF16)
        own[2 * j, :W] = grad[:, :128]
        own[2 * j + 1, :W] = grad[:, 128:]
        core_copy(i).start()

    def core_add(i):
        core_copy(i).wait_recv()
        tiles = pl.ds(2 * piece(i), 2)
        other[tiles] = (other[tiles].astype(F32) + own[tiles, half].astype(F32)).astype(BF16)

    for i in range(4):
        relation_piece(i)
        if i:
            core_add(i - 1)
            x_copy(i - 1).start()
    core_add(3)

    def rows_step(c, table, state, hi_ref, lo_ref, oh, low, wts):
        here = aligned(c, CHUNK)
        grad = dot(hi_ref[...], oh[here, :], NT) + dot(lo_ref[...], oh[here, :], NT) + dot(low[...], wts[here, :], NT)
        return here, update(table[:, here].astype(F32), state[:, here], grad)

    def target_copy(c):
        here = aligned(c, CHUNK)
        return send(tgt_new.at[:, here], tgt_out.at[:, here], t_s.at[c], t_r.at[c], "y", 2)

    def target_step(c, _):
        here, (new, new_state) = rows_step(c, tgt_ref, tgt_state, gt_hi, gt_lo, oh_d, q_low, w_t)
        tgt_new[:, here] = new.astype(BF16)
        tgt_state_new[:, here] = new_state
        return 0

    def source_step(c, _):
        here, (new, new_state) = rows_step(c, src_ref, src_state, gs_hi, gs_lo, oh_s, p_low, w_s)
        src_out[:, here] = new.astype(BF16)
        src_state_out[:, here] = new_state
        return 0

    def target_first(c, _):
        target_step(c, 0)
        target_copy(c).start()
        return 0

    lax.fori_loop(0, 2, target_first, 0)
    for i in range(3):
        x_copy(i).wait_recv()
    mine = pl.ds(2 * x, 2)
    at_z[:, :PART] = (
        other[mine].astype(F32) + from_x[0].astype(F32) + from_x[1].astype(F32) + from_x[2].astype(F32)
    ).astype(BF16)
    z_hops, y_hops = HOPS["z"], HOPS["y"]
    z_copies = []
    for i, hop in enumerate(z_hops):
        to = lax.rem(z + hop, 8)
        z_copies.append(send(at_z.at[to // 4, aligned(to % 4, 64)], from_z.at[i], z_s.at[i], z_r.at[i], "z", hop))
        z_copies[-1].start()
    lax.fori_loop(2, 4, target_step, 0)
    for copy in z_copies:
        copy.wait_recv()
    summed = at_z[z // 4, aligned(z % 4, 64), :].astype(F32)
    for i in range(7):
        summed = summed + from_z[i].astype(F32)
    from_y[y] = summed.astype(BF16)
    y_copies = []
    for i, hop in enumerate(y_hops):
        y_copies.append(send(from_y.at[y], from_y.at[y], y_s.at[i], y_r.at[i], "y", hop))
        y_copies[-1].start()
    lax.fori_loop(0, 1, source_step, 0)
    for copy in y_copies:
        copy.wait_recv()
    target_copy(2).start()
    target_copy(3).start()
    state_copy = send(tgt_state_new, tgt_state_out, ts_s, ts_r, "y", 2)
    state_copy.start()
    summed = from_y[0].astype(F32) + from_y[1].astype(F32) + from_y[2].astype(F32) + from_y[3].astype(F32)
    got_y[...] = summed.astype(BF16)
    slot = got.at[core, x, z // 4, aligned(z % 4, 64)]
    back_z = []
    for i, hop in enumerate(z_hops):
        back_z.append(send(got_y, slot, gz_s.at[i], gz_r.at[i], "z", hop))
        back_z[-1].start()
    got[core, x, z // 4, aligned(z % 4, 64), :] = got_y[...]
    lax.fori_loop(1, 3, source_step, 0)
    for copy in back_z:
        copy.wait_recv()

    def piece_copy(index, send_sem, recv_sem, axis, hop):
        ready = got.at[core, index, :, pl.ds(0, PART)]
        return send(ready, ready, send_sem, recv_sem, axis, hop)

    back_x = []
    for i, hop in enumerate(HOPS["x"]):
        back_x.append(piece_copy(x, gx_s.at[i], gx_r.at[i], "x", hop))
        back_x[-1].start()
    arrival = (x,) + tuple(lax.rem(x + 4 - hop, 4) for hop in HOPS["x"])
    cores = [piece_copy(x, gc_s.at[0], gc_r.at[0], "core", 1)]
    cores[0].start()
    lax.fori_loop(3, 4, source_step, 0)

    def relation_rows(i):
        cores[i].wait_recv()
        j = arrival[i]
        for half_tile in range(2):
            here = aligned(2 * j + half_tile, 128)
            grad = jnp.concatenate([got[0, j, half_tile, :PART], got[1, j, half_tile, : W - PART]], axis=0).astype(F32)
            new, new_state = update(rel_ref[:, here], rel_state[:, here], grad)
            rel_out[:, here] = new
            rel_state_out[:, here] = new_state

    for i in range(3):
        back_x[i].wait_recv()
        cores.append(piece_copy(arrival[i + 1], gc_s.at[i + 1], gc_r.at[i + 1], "core", 1))
        cores[-1].start()
        relation_rows(i)
    relation_rows(3)
    for i in range(4):
        core_copy(i).wait_send()
        target_copy(i).wait()
    for i in range(3):
        x_copy(i).wait_send()
    for copy in z_copies + y_copies + back_z + back_x + cores:
        copy.wait_send()
    state_copy.wait()


def finish_kernel(*refs):
    ins, outs, stages, in_sem, out_sem = refs[:6], refs[6:12], refs[12:18], refs[18], refs[19]
    loads, stores = [], []
    for half in range(2):
        for i, (here, stage, there) in enumerate(zip(ins, stages, outs)):
            if half and here.shape[0] == 1:
                continue
            rows = pl.ds(0, 1) if here.shape[0] == 1 else pl.ds(half * 208, 192 if half else 208)
            loads.append(pltpu.make_async_copy(here.at[rows], stage.at[rows], in_sem.at[half, i]))
            stores.append(pltpu.make_async_copy(stage.at[rows], there.at[rows], out_sem.at[half, i]))
    for load in loads:
        load.start()
    for load, store in zip(loads, stores):
        load.wait()
        store.start()
    for store in stores:
        store.wait()


def shards(src, src_state, tgt, tgt_state, rel, rel_state, sid, rid, did, sneg, tneg, live):
    vm = pl.BlockSpec(memory_space=pltpu.VMEM)
    sm = pl.BlockSpec(memory_space=pltpu.SMEM)
    hbm = pl.BlockSpec(memory_space=pltpu.HBM)
    shape = jax.ShapeDtypeStruct
    dma = pltpu.SemaphoreType.DMA

    def vmem(*dims, dtype=BF16):
        return pltpu.VMEM(dims, dtype)

    def like(ref):
        return pltpu.VMEM(ref.shape, ref.dtype)

    rows_bf, row_f = shape((W, ROWS), BF16), shape((1, ROWS), F32)
    rows_f, ids, negs = shape((W, ROWS), F32), shape((1, EDGES), jnp.int32), shape(sneg.shape, jnp.int32)
    wide = [(1, ROWS), (1, EDGES)]
    results = (rows_bf, row_f, rows_bf, row_f, rows_f, row_f)
    outs = pl.pallas_call(
        bucket_kernel,
        out_shape=results,
        in_specs=[sm] + [hbm] * 11,
        out_specs=[vm] * 6,
        scratch_shapes=[like(r) for r in (*results, ids, ids, ids, negs, negs)]
        + [dma((11,)), vmem(ROWS, W), vmem(ROWS, W)]
        + [vmem(ROWS, EDGES)] * 5
        + [vmem(W, EDGES)] * 7
        + [
            vmem(W, ROWS), vmem(1, ROWS, dtype=F32), vmem(8, 2 * PART, 128), vmem(8, PART, 128),
            vmem(3, 2, PART, 128), vmem(2, 256, 128), vmem(7, 64, 128), vmem(4, 64, 128), vmem(64, 128),
            vmem(2, 4, 2, 256, 128),
        ]
        + [dma((n,)) for n in (4, 4, 3, 3, 7, 7, 3, 3, 7, 7, 3, 3, 4, 4, 4, 4)]
        + [dma(()), dma(())],
        compiler_params=pltpu.CompilerParams(
            collective_id=0, has_side_effects=True, vmem_limit_bytes=60 * 2**20
        ),
        name="bucket",
    )(live, src.T, src_state.reshape(wide[0]), tgt.T, tgt_state.reshape(wide[0]), rel.T, rel_state.reshape(wide[0]),
      sid.reshape(wide[1]), rid.reshape(wide[1]), did.reshape(wide[1]), sneg, tneg)
    outs = pl.pallas_call(
        finish_kernel,
        out_shape=results,
        in_specs=[hbm] * 6,
        out_specs=[hbm] * 6,
        scratch_shapes=[like(r) for r in results] + [dma((2, 6)), dma((2, 6))],
        compiler_params=pltpu.CompilerParams(vmem_limit_bytes=60 * 2**20),
        name="finish",
    )(*outs)
    return (outs[0].T, outs[1].reshape(ROWS), outs[2].T, outs[3].reshape(ROWS), outs[4].T, outs[5].reshape(ROWS))


def solution(mesh):
    split_rows, split_one, copied = P(("blk", "grp"), None), P(("blk", "grp")), P()
    return jax.shard_map(
        shards,
        mesh=mesh,
        in_specs=(split_rows, split_one, split_rows, split_one, copied, copied,
                  split_one, split_one, split_one, split_rows, split_rows, split_one),
        out_specs=(split_rows, split_one, split_rows, split_one, copied, copied),
        check_vma=False,
    )
```

```python
import jax
import jax.numpy as jnp
from jax import lax
from jax.experimental import pallas as pl
from jax.experimental.pallas import tpu as pltpu
from jax.sharding import PartitionSpec as P

F32, BF16 = jnp.float32, jnp.bfloat16
W, HALF, ROWS, EDGES, BLOCK, NEG = 400, 200, 1024, 2048, 128, 1024
CHUNK = 256
EDGE_CHUNK = 1024
LANE_ROWS = 320
PART = 208
RATE = 0.1
NN = (((1,), (0,)), ((), ()))
NT = (((1,), (1,)), ((), ()))
MESH = pl.DeviceIdType.MESH
SIZE = {"y": 4, "x": 4, "z": 8, "core": 2}
HOPS = {"y": (2, 1, 3), "x": (2, 1, 3), "z": (4, 3, 5, 2, 6, 1, 7), "core": (1,)}


def place():
    blk, grp = lax.axis_index("blk"), lax.axis_index("grp")
    return {"y": blk // 16, "x": blk // 4 % 4, "z": grp * 2 + blk // 2 % 2, "core": blk % 2}


def peer(me, axis, hop):
    at = dict(me)
    at[axis] = lax.rem(me[axis] + hop, SIZE[axis])
    return (at["y"] * 16 + at["x"] * 4 + at["z"] % 2 * 2 + at["core"], at["z"] // 2)


def dot(a, b, dims=NN):
    return lax.dot_general(a, b, dims, preferred_element_type=F32)


def mul(a, b):
    ar, ai, br, bi = a[:HALF], a[HALF:], b[:HALF], b[HALF:]
    return jnp.concatenate([ar * br - ai * bi, ar * bi + ai * br], axis=0)


def mulc(a, b):
    ar, ai, br, bi = a[:HALF], a[HALF:], b[:HALF], b[HALF:]
    return jnp.concatenate([ar * br + ai * bi, ai * br - ar * bi], axis=0)


def split(x):
    hi = x.astype(BF16)
    return hi, (x - hi.astype(F32)).astype(BF16)


def one_hot(ids, count):
    at = lax.broadcasted_iota(jnp.int32, (count, ids.shape[1]), 0)
    return jnp.where(at == ids, 1.0, 0.0).astype(BF16)


def pick(table, ids, rows):
    low, high = ids % 128, ids // 128
    parts = []
    for b in range(ids.shape[1] // 128):
        lanes = slice(128 * b, 128 * b + 128)
        at = jnp.broadcast_to(low[:, lanes], (rows, 128))
        tile = jnp.broadcast_to(high[:, lanes], (rows, 128))
        out = jnp.take_along_axis(table[:rows, :128], at, axis=1, mode="promise_in_bounds")
        for t in range(1, ROWS // 128):
            got = jnp.take_along_axis(table[:rows, 128 * t : 128 * t + 128], at, axis=1, mode="promise_in_bounds")
            out = jnp.where(tile == t, got, out)
        parts.append(out)
    return jnp.concatenate(parts, axis=1)


def counts_of(ids, scale):
    grid = dot(one_hot(ids % 32, 32), one_hot(ids // 32, 32), NT) * scale
    return jnp.concatenate([jnp.broadcast_to(grid[:, h : h + 1], (32, BLOCK)) for h in range(32)], axis=0)


def weights_of(scores, count):
    return (count + count * jnp.tanh(scores)).astype(BF16)


def update(table, state, grad):
    new_state = state + jnp.sum(grad * grad, axis=0, keepdims=True) * (1.0 / W)
    return table - RATE * grad * lax.rsqrt(new_state), new_state


def aligned(index, size):
    return pl.ds(pl.multiple_of(index * size, size), size)


def bucket_kernel(
    live_ref, src_h, src_state_h, tgt_h, tgt_state_h, rel_h, rel_state_h, sid_h, rid_h, did_h, sneg_h, tneg_h,
    src_out, src_state_out, tgt_out, tgt_state_out, rel_out, rel_state_out,
    src_ref, src_state, tgt_ref, tgt_state, rel_ref, rel_state, sid_ref, rid_ref, did_ref, sneg_ref, tneg_ref, in_sem,
    src_t, tgt_t, rel_hl, oh_s, oh_d, oh_r, w_s, w_t, q_low, p_low, gs_hi, gs_lo, gt_hi, gt_lo, rt,
    own, other, from_x, at_z, from_z, from_y, got_y, got,
    core_s, core_r, x_s, x_r, z_s, z_r, y_s, y_r, gz_s, gz_r, gx_s, gx_r, gc_s, gc_r,
    t_s, t_r, so_sem, ro_sem, ts_s, ts_r, state_sem,
):
    loads = [
        pltpu.make_async_copy(here, there, in_sem.at[i])
        for i, (here, there) in enumerate([
            (src_h, src_ref), (tgt_h, tgt_ref), (rel_h, rel_ref), (sid_h, sid_ref), (rid_h, rid_ref), (did_h, did_ref),
            (sneg_h, sneg_ref), (tneg_h, tneg_ref), (src_state_h, src_state), (tgt_state_h, tgt_state),
            (rel_state_h, rel_state),
        ])
    ]
    for load in loads:
        load.start()
    me = place()
    core, x, y, z = me["core"], me["x"], me["y"], me["z"]
    barrier = pltpu.get_barrier_semaphore()
    total = 0
    for axis, hops in HOPS.items():
        for hop in hops:
            pl.semaphore_signal(barrier, inc=1, device_id=peer(me, axis, hop), device_id_type=MESH)
            total += 1

    def send(src, dst, send_sem, recv_sem, axis, hop):
        return pltpu.make_async_remote_copy(
            src_ref=src, dst_ref=dst, send_sem=send_sem, recv_sem=recv_sem,
            device_id=peer(me, axis, hop), device_id_type=MESH,
        )

    own[:, W:] = jnp.zeros((8, 2 * PART - W, 128), BF16)
    at_z[:, PART:] = jnp.zeros((2, 256 - PART, 128), BF16)
    loads[0].wait()
    src_t[...] = (0.5 * src_ref[...].astype(F32)).T.astype(BF16)
    loads[1].wait()
    tgt_t[...] = (0.5 * tgt_ref[...].astype(F32)).T.astype(BF16)
    for load in loads[2:]:
        load.wait()
    rel_hl[: W - LANE_ROWS], rel_hl[W - LANE_ROWS :] = split(rel_ref[LANE_ROWS:])
    count = live_ref[0]

    def edges(c, _):
        first = pl.multiple_of(c * EDGE_CHUNK, EDGE_CHUNK)
        here = pl.ds(first, EDGE_CHUNK)
        slots = first + lax.broadcasted_iota(jnp.int32, (1, EDGE_CHUNK), 1)
        alive = jnp.where(slots < count, 1.0, 0.0).astype(F32)

        def block_counts(negs):
            blocks = []
            for i in range(EDGE_CHUNK // BLOCK):
                scale = jnp.where(first + i * BLOCK < count, 0.5 / NEG, 0.0).astype(F32)
                blocks.append(counts_of(negs[pl.ds(c * (EDGE_CHUNK // BLOCK) + i, 1), :], scale))
            return jnp.concatenate(blocks, axis=1)

        ohs = one_hot(sid_ref[:, here], ROWS)
        ohd = one_hot(did_ref[:, here], ROWS)
        ohr = one_hot(rid_ref[:, here], ROWS)
        oh_s[:, here] = ohs
        oh_d[:, here] = ohd
        oh_r[:, here] = ohr
        s = dot(src_ref[...], ohs)
        d = dot(tgt_ref[...], ohd)
        low = dot(rel_hl[...], ohr)
        r = jnp.concatenate(
            [pick(rel_ref, rid_ref[:, here], LANE_ROWS), low[: W - LANE_ROWS] + low[W - LANE_ROWS :]], axis=0
        )
        q = mul(s, r)
        p = mulc(r, d)
        pos = jnp.sum(q * d, axis=0, keepdims=True)
        pos_grad = -alive / (1.0 + jnp.exp(pos))
        ql = q.astype(BF16)
        plow = p.astype(BF16)
        q_low[:, here] = ql
        p_low[:, here] = plow
        wt = weights_of(dot(tgt_t[...], ql), block_counts(tneg_ref))
        w_t[:, here] = wt
        ws = weights_of(dot(src_t[...], plow), block_counts(sneg_ref))
        w_s[:, here] = ws
        qg = pos_grad * d + dot(tgt_ref[...], wt)
        pg = dot(src_ref[...], ws)
        gs_hi[:, here], gs_lo[:, here] = split(mulc(qg, r))
        gt_hi[:, here], gt_lo[:, here] = split(pos_grad * q + mul(pg, r))
        rt[:, here] = (mulc(qg, s) + mulc(d, pg)).astype(BF16)
        return 0

    lax.fori_loop(0, EDGES // EDGE_CHUNK, edges, 0)
    pl.semaphore_wait(barrier, total)

    half = aligned(core, PART)
    far = aligned(1 - core, PART)
    order = HOPS["x"] + (0,)

    def piece(i):
        return lax.rem(x + order[i], 4)

    def core_copy(i):
        tiles = pl.ds(2 * piece(i), 2)
        return send(own.at[tiles, far], other.at[tiles], core_s.at[i], core_r.at[i], "core", 1)

    def x_copy(i):
        return send(other.at[pl.ds(2 * piece(i), 2)], from_x.at[i], x_s.at[i], x_r.at[i], "x", order[i])

    def relation_piece(i):
        j = piece(i)
        grad = dot(rt[...], oh_r[aligned(j, CHUNK), :], NT).astype(BF16)
        own[2 * j, :W] = grad[:, :128]
        own[2 * j + 1, :W] = grad[:, 128:]
        core_copy(i).start()

    def core_add(i):
        core_copy(i).wait_recv()
        tiles = pl.ds(2 * piece(i), 2)
        other[tiles] = (other[tiles].astype(F32) + own[tiles, half].astype(F32)).astype(BF16)

    for i in range(4):
        relation_piece(i)
        if i:
            core_add(i - 1)
            x_copy(i - 1).start()
    core_add(3)

    def rows_step(c, table, state, hi_ref, lo_ref, oh, low, wts):
        here = aligned(c, CHUNK)
        grad = dot(hi_ref[...], oh[here, :], NT) + dot(lo_ref[...], oh[here, :], NT) + dot(low[...], wts[here, :], NT)
        return here, update(table[:, here].astype(F32), state[:, here], grad)

    def target_copy(c):
        here = aligned(c, CHUNK)
        return send(tgt_ref.at[:, here], tgt_out.at[:, here], t_s.at[c], t_r.at[c], "y", 2)

    def target_step(c, _):
        here, (new, new_state) = rows_step(c, tgt_ref, tgt_state, gt_hi, gt_lo, oh_d, q_low, w_t)
        tgt_ref[:, here] = new.astype(BF16)
        tgt_state[:, here] = new_state
        return 0

    def source_copy(c):
        here = aligned(c, CHUNK)
        return pltpu.make_async_copy(src_ref.at[:, here], src_out.at[:, here], so_sem.at[c])

    def source_step(c, _):
        here, (new, new_state) = rows_step(c, src_ref, src_state, gs_hi, gs_lo, oh_s, p_low, w_s)
        src_ref[:, here] = new.astype(BF16)
        src_state[:, here] = new_state
        source_copy(c).start()
        return 0

    def target_first(c, _):
        target_step(c, 0)
        target_copy(c).start()
        return 0

    lax.fori_loop(0, 2, target_first, 0)
    for i in range(3):
        x_copy(i).wait_recv()
    mine = pl.ds(2 * x, 2)
    at_z[:, :PART] = (
        other[mine].astype(F32) + from_x[0].astype(F32) + from_x[1].astype(F32) + from_x[2].astype(F32)
    ).astype(BF16)
    z_hops, y_hops = HOPS["z"], HOPS["y"]
    z_copies = []
    for i, hop in enumerate(z_hops):
        to = lax.rem(z + hop, 8)
        z_copies.append(send(at_z.at[to // 4, aligned(to % 4, 64)], from_z.at[i], z_s.at[i], z_r.at[i], "z", hop))
        z_copies[-1].start()
    lax.fori_loop(2, 4, target_step, 0)
    for copy in z_copies:
        copy.wait_recv()
    summed = at_z[z // 4, aligned(z % 4, 64), :].astype(F32)
    for i in range(7):
        summed = summed + from_z[i].astype(F32)
    from_y[y] = summed.astype(BF16)
    y_copies = []
    for i, hop in enumerate(y_hops):
        y_copies.append(send(from_y.at[y], from_y.at[y], y_s.at[i], y_r.at[i], "y", hop))
        y_copies[-1].start()
    lax.fori_loop(0, 1, source_step, 0)
    for copy in y_copies:
        copy.wait_recv()
    target_copy(2).start()
    target_copy(3).start()
    state_copy = send(tgt_state, tgt_state_out, ts_s, ts_r, "y", 2)
    state_copy.start()
    summed = from_y[0].astype(F32) + from_y[1].astype(F32) + from_y[2].astype(F32) + from_y[3].astype(F32)
    got_y[...] = summed.astype(BF16)
    slot = got.at[core, x, z // 4, aligned(z % 4, 64)]
    back_z = []
    for i, hop in enumerate(z_hops):
        back_z.append(send(got_y, slot, gz_s.at[i], gz_r.at[i], "z", hop))
        back_z[-1].start()
    got[core, x, z // 4, aligned(z % 4, 64), :] = got_y[...]
    lax.fori_loop(1, 3, source_step, 0)
    for copy in back_z:
        copy.wait_recv()

    def piece_copy(index, send_sem, recv_sem, axis, hop):
        ready = got.at[core, index, :, pl.ds(0, PART)]
        return send(ready, ready, send_sem, recv_sem, axis, hop)

    back_x = []
    for i, hop in enumerate(HOPS["x"]):
        back_x.append(piece_copy(x, gx_s.at[i], gx_r.at[i], "x", hop))
        back_x[-1].start()
    arrival = (x,) + tuple(lax.rem(x + 4 - hop, 4) for hop in HOPS["x"])
    cores = [piece_copy(x, gc_s.at[0], gc_r.at[0], "core", 1)]
    cores[0].start()
    lax.fori_loop(3, 4, source_step, 0)

    source_state_copy = pltpu.make_async_copy(src_state, src_state_out, state_sem.at[0])
    source_state_copy.start()

    def relation_copy(i):
        here = aligned(arrival[i], CHUNK)
        return pltpu.make_async_copy(rel_ref.at[:, here], rel_out.at[:, here], ro_sem.at[i])

    def relation_rows(i):
        cores[i].wait_recv()
        j = arrival[i]
        for half_tile in range(2):
            here = aligned(2 * j + half_tile, 128)
            grad = jnp.concatenate([got[0, j, half_tile, :PART], got[1, j, half_tile, : W - PART]], axis=0).astype(F32)
            new, new_state = update(rel_ref[:, here], rel_state[:, here], grad)
            rel_ref[:, here] = new
            rel_state[:, here] = new_state
        relation_copy(i).start()

    for i in range(3):
        back_x[i].wait_recv()
        cores.append(piece_copy(arrival[i + 1], gc_s.at[i + 1], gc_r.at[i + 1], "core", 1))
        cores[-1].start()
        relation_rows(i)
    relation_rows(3)
    relation_state_copy = pltpu.make_async_copy(rel_state, rel_state_out, state_sem.at[1])
    relation_state_copy.start()
    source_state_copy.wait()
    for i in range(4):
        source_copy(i).wait()
        core_copy(i).wait_send()
        target_copy(i).wait()
    for i in range(3):
        x_copy(i).wait_send()
    for copy in z_copies + y_copies + back_z + back_x + cores:
        copy.wait_send()
    state_copy.wait()
    for i in range(4):
        relation_copy(i).wait()
    relation_state_copy.wait()


def finish_kernel(*refs):
    ins, outs, stages, in_sem, out_sem = refs[:6], refs[6:12], refs[12:18], refs[18], refs[19]
    loads, stores = [], []
    for part in range(2):
        for i, (here, stage, there) in enumerate(zip(ins, stages, outs)):
            if here.shape[0] == 1:
                if part:
                    continue
                rows = pl.ds(0, 1)
            else:
                rows = pl.ds(part * 208, 192 if part else 208)
            loads.append(pltpu.make_async_copy(here.at[rows], stage.at[rows], in_sem.at[part, i]))
            stores.append(pltpu.make_async_copy(stage.at[rows], there.at[rows], out_sem.at[part, i]))
    for load in loads:
        load.start()
    for load, store in zip(loads, stores):
        load.wait()
        store.start()
    for store in stores:
        store.wait()


def shards(src, src_state, tgt, tgt_state, rel, rel_state, sid, rid, did, sneg, tneg, live):
    sm = pl.BlockSpec(memory_space=pltpu.SMEM)
    hbm = pl.BlockSpec(memory_space=pltpu.HBM)
    shape = jax.ShapeDtypeStruct
    dma = pltpu.SemaphoreType.DMA

    def vmem(*dims, dtype=BF16):
        return pltpu.VMEM(dims, dtype)

    def like(ref):
        return pltpu.VMEM(ref.shape, ref.dtype)

    rows_bf, row_f = shape((W, ROWS), BF16), shape((1, ROWS), F32)
    rows_f, ids, negs = shape((W, ROWS), F32), shape((1, EDGES), jnp.int32), shape(sneg.shape, jnp.int32)
    wide = [(1, ROWS), (1, EDGES)]
    results = (rows_bf, row_f, rows_bf, row_f, rows_f, row_f)
    outs = pl.pallas_call(
        bucket_kernel,
        out_shape=results,
        in_specs=[sm] + [hbm] * 11,
        out_specs=[hbm] * 6,
        scratch_shapes=[like(r) for r in (*results, ids, ids, ids, negs, negs)]
        + [dma((11,)), vmem(ROWS, W), vmem(ROWS, W), vmem(2 * (W - LANE_ROWS), ROWS)]
        + [vmem(ROWS, EDGES)] * 5
        + [vmem(W, EDGES)] * 7
        + [
            vmem(8, 2 * PART, 128), vmem(8, PART, 128),
            vmem(3, 2, PART, 128), vmem(2, 256, 128), vmem(7, 64, 128), vmem(4, 64, 128), vmem(64, 128),
            vmem(2, 4, 2, 256, 128),
        ]
        + [dma((n,)) for n in (4, 4, 3, 3, 7, 7, 3, 3, 7, 7, 3, 3, 4, 4, 4, 4, 4, 4)]
        + [dma(()), dma(()), dma((2,))],
        compiler_params=pltpu.CompilerParams(
            collective_id=0, has_side_effects=True, vmem_limit_bytes=60 * 2**20
        ),
        name="bucket",
    )(live, src.T, src_state.reshape(wide[0]), tgt.T, tgt_state.reshape(wide[0]), rel.T, rel_state.reshape(wide[0]),
      sid.reshape(wide[1]), rid.reshape(wide[1]), did.reshape(wide[1]), sneg, tneg)
    outs = pl.pallas_call(
        finish_kernel,
        out_shape=results,
        in_specs=[hbm] * 6,
        out_specs=[hbm] * 6,
        scratch_shapes=[like(r) for r in results] + [dma((2, 6)), dma((2, 6))],
        compiler_params=pltpu.CompilerParams(vmem_limit_bytes=60 * 2**20),
        name="finish",
    )(*outs)
    return (outs[0].T, outs[1].reshape(ROWS), outs[2].T, outs[3].reshape(ROWS), outs[4].T, outs[5].reshape(ROWS))


def solution(mesh):
    split_rows, split_one, copied = P(("blk", "grp"), None), P(("blk", "grp")), P()
    return jax.shard_map(
        shards,
        mesh=mesh,
        in_specs=(split_rows, split_one, split_rows, split_one, copied, copied,
                  split_one, split_one, split_one, split_rows, split_rows, split_one),
        out_specs=(split_rows, split_one, split_rows, split_one, copied, copied),
        check_vma=False,
    )
```

```python
import jax
import jax.numpy as jnp
from jax import lax
from jax.experimental import pallas as pl
from jax.experimental.pallas import tpu as pltpu
from jax.sharding import PartitionSpec as P

F32, BF16 = jnp.float32, jnp.bfloat16
W, HALF, ROWS, EDGES, BLOCK, NEG = 400, 200, 1024, 2048, 128, 1024
CHUNK = 256
EDGE_CHUNK = 1024
LANE_ROWS = 320
PART = 208
RATE = 0.1
NN = (((1,), (0,)), ((), ()))
NT = (((1,), (1,)), ((), ()))
MESH = pl.DeviceIdType.MESH
SIZE = {"y": 4, "x": 4, "z": 8, "core": 2}
HOPS = {"y": (2, 1, 3), "x": (2, 1, 3), "z": (4, 3, 5, 2, 6, 1, 7), "core": (1,)}


def place():
    blk, grp = lax.axis_index("blk"), lax.axis_index("grp")
    return {"y": blk // 16, "x": blk // 4 % 4, "z": grp * 2 + blk // 2 % 2, "core": blk % 2}


def peer(me, axis, hop):
    at = dict(me)
    at[axis] = lax.rem(me[axis] + hop, SIZE[axis])
    return (at["y"] * 16 + at["x"] * 4 + at["z"] % 2 * 2 + at["core"], at["z"] // 2)


def dot(a, b, dims=NN):
    return lax.dot_general(a, b, dims, preferred_element_type=F32)


def mul(a, b):
    ar, ai, br, bi = a[:HALF], a[HALF:], b[:HALF], b[HALF:]
    return jnp.concatenate([ar * br - ai * bi, ar * bi + ai * br], axis=0)


def mulc(a, b):
    ar, ai, br, bi = a[:HALF], a[HALF:], b[:HALF], b[HALF:]
    return jnp.concatenate([ar * br + ai * bi, ai * br - ar * bi], axis=0)


def split(x):
    hi = x.astype(BF16)
    return hi, (x - hi.astype(F32)).astype(BF16)


def one_hot(ids, count):
    at = lax.broadcasted_iota(jnp.int32, (count, ids.shape[1]), 0)
    return jnp.where(at == ids, 1.0, 0.0).astype(BF16)


def pick(table, ids, rows):
    low, high = ids % 128, ids // 128
    parts = []
    for b in range(ids.shape[1] // 128):
        lanes = slice(128 * b, 128 * b + 128)
        at = jnp.broadcast_to(low[:, lanes], (rows, 128))
        tile = jnp.broadcast_to(high[:, lanes], (rows, 128))
        out = jnp.take_along_axis(table[:rows, :128], at, axis=1, mode="promise_in_bounds")
        for t in range(1, ROWS // 128):
            got = jnp.take_along_axis(table[:rows, 128 * t : 128 * t + 128], at, axis=1, mode="promise_in_bounds")
            out = jnp.where(tile == t, got, out)
        parts.append(out)
    return jnp.concatenate(parts, axis=1)


def counts_of(ids, scale):
    grid = dot(one_hot(ids % 32, 32), one_hot(ids // 32, 32), NT) * scale
    return jnp.concatenate([jnp.broadcast_to(grid[:, h : h + 1], (32, BLOCK)) for h in range(32)], axis=0)


def weights_of(scores, count):
    return (count + count * jnp.tanh(scores)).astype(BF16)


def update(table, state, grad):
    new_state = state + jnp.sum(grad * grad, axis=0, keepdims=True) * (1.0 / W)
    return table - RATE * grad * lax.rsqrt(new_state), new_state


def aligned(index, size):
    return pl.ds(pl.multiple_of(index * size, size), size)


def bucket_kernel(
    live_ref, src_h, src_state_h, tgt_h, tgt_state_h, rel_h, rel_state_h, sid_h, rid_h, did_h, sneg_h, tneg_h,
    src_out, src_state_out, tgt_out, tgt_state_out, rel_out, rel_state_out,
    src_ref, src_state, tgt_ref, tgt_state, rel_ref, rel_state, sid_ref, rid_ref, did_ref, sneg_ref, tneg_ref, in_sem,
    src_t, tgt_t, rel_hl, oh_s, oh_d, oh_r, w_s, w_t, q_low, p_low, gs_hi, gs_lo, gt_hi, gt_lo, rt,
    own, other, from_x, at_z, from_z, from_y, got_y, got,
    core_s, core_r, x_s, x_r, z_s, z_r, y_s, y_r, gz_s, gz_r, gx_s, gx_r, gc_s, gc_r,
    t_s, t_r, so_sem, ro_sem, ts_s, ts_r, state_sem,
):
    loads = [
        pltpu.make_async_copy(here, there, in_sem.at[i])
        for i, (here, there) in enumerate([
            (src_h, src_ref), (tgt_h, tgt_ref), (rel_h, rel_ref), (sid_h, sid_ref), (rid_h, rid_ref), (did_h, did_ref),
            (sneg_h, sneg_ref), (tneg_h, tneg_ref), (src_state_h, src_state), (tgt_state_h, tgt_state),
            (rel_state_h, rel_state),
        ])
    ]
    for load in loads:
        load.start()
    me = place()
    core, x, y, z = me["core"], me["x"], me["y"], me["z"]
    barrier = pltpu.get_barrier_semaphore()
    total = 0
    for axis, hops in HOPS.items():
        for hop in hops:
            pl.semaphore_signal(barrier, inc=1, device_id=peer(me, axis, hop), device_id_type=MESH)
            total += 1

    def send(src, dst, send_sem, recv_sem, axis, hop):
        return pltpu.make_async_remote_copy(
            src_ref=src, dst_ref=dst, send_sem=send_sem, recv_sem=recv_sem,
            device_id=peer(me, axis, hop), device_id_type=MESH,
        )

    own[:, W:] = jnp.zeros((8, 2 * PART - W, 128), BF16)
    at_z[:, PART:] = jnp.zeros((2, 256 - PART, 128), BF16)
    loads[0].wait()
    src_t[...] = (0.5 * src_ref[...].astype(F32)).T.astype(BF16)
    loads[1].wait()
    tgt_t[...] = (0.5 * tgt_ref[...].astype(F32)).T.astype(BF16)
    for load in loads[2:]:
        load.wait()
    rel_hl[: W - LANE_ROWS], rel_hl[W - LANE_ROWS :] = split(rel_ref[LANE_ROWS:])
    count = live_ref[0]

    def edges(c, _):
        first = pl.multiple_of(c * EDGE_CHUNK, EDGE_CHUNK)
        here = pl.ds(first, EDGE_CHUNK)
        slots = first + lax.broadcasted_iota(jnp.int32, (1, EDGE_CHUNK), 1)
        alive = jnp.where(slots < count, 1.0, 0.0).astype(F32)

        def block_counts(negs):
            blocks = []
            for i in range(EDGE_CHUNK // BLOCK):
                scale = jnp.where(first + i * BLOCK < count, 0.5 / NEG, 0.0).astype(F32)
                blocks.append(counts_of(negs[pl.ds(c * (EDGE_CHUNK // BLOCK) + i, 1), :], scale))
            return jnp.concatenate(blocks, axis=1)

        ohs = one_hot(sid_ref[:, here], ROWS)
        ohd = one_hot(did_ref[:, here], ROWS)
        ohr = one_hot(rid_ref[:, here], ROWS)
        oh_s[:, here] = ohs
        oh_d[:, here] = ohd
        oh_r[:, here] = ohr
        s = dot(src_ref[...], ohs)
        d = dot(tgt_ref[...], ohd)
        low = dot(rel_hl[...], ohr)
        r = jnp.concatenate(
            [pick(rel_ref, rid_ref[:, here], LANE_ROWS), low[: W - LANE_ROWS] + low[W - LANE_ROWS :]], axis=0
        )
        q = mul(s, r)
        p = mulc(r, d)
        pos = jnp.sum(q * d, axis=0, keepdims=True)
        pos_grad = -alive / (1.0 + jnp.exp(pos))
        ql = q.astype(BF16)
        plow = p.astype(BF16)
        q_low[:, here] = ql
        p_low[:, here] = plow
        wt = weights_of(dot(tgt_t[...], ql), block_counts(tneg_ref))
        w_t[:, here] = wt
        ws = weights_of(dot(src_t[...], plow), block_counts(sneg_ref))
        w_s[:, here] = ws
        qg = pos_grad * d + dot(tgt_ref[...], wt)
        pg = dot(src_ref[...], ws)
        gs_hi[:, here], gs_lo[:, here] = split(mulc(qg, r))
        gt_hi[:, here], gt_lo[:, here] = split(pos_grad * q + mul(pg, r))
        rt[:, here] = (mulc(qg, s) + mulc(d, pg)).astype(BF16)
        return 0

    lax.fori_loop(0, EDGES // EDGE_CHUNK, edges, 0)
    pl.semaphore_wait(barrier, total)

    half = aligned(core, PART)
    far = aligned(1 - core, PART)
    order = HOPS["x"] + (0,)

    def piece(i):
        return lax.rem(x + order[i], 4)

    def core_copy(i):
        tiles = pl.ds(2 * piece(i), 2)
        return send(own.at[tiles, far], other.at[tiles], core_s.at[i], core_r.at[i], "core", 1)

    def x_copy(i):
        return send(other.at[pl.ds(2 * piece(i), 2)], from_x.at[i], x_s.at[i], x_r.at[i], "x", order[i])

    def relation_piece(i):
        j = piece(i)
        grad = dot(rt[...], oh_r[aligned(j, CHUNK), :], NT).astype(BF16)
        own[2 * j, :W] = grad[:, :128]
        own[2 * j + 1, :W] = grad[:, 128:]
        core_copy(i).start()

    def core_add(i):
        core_copy(i).wait_recv()
        tiles = pl.ds(2 * piece(i), 2)
        other[tiles] = (other[tiles].astype(F32) + own[tiles, half].astype(F32)).astype(BF16)

    for i in range(4):
        relation_piece(i)
        if i:
            core_add(i - 1)
            x_copy(i - 1).start()
    core_add(3)

    def rows_step(c, table, state, hi_ref, lo_ref, oh, low, wts):
        here = aligned(c, CHUNK)
        grad = dot(hi_ref[...], oh[here, :], NT) + dot(lo_ref[...], oh[here, :], NT) + dot(low[...], wts[here, :], NT)
        return here, update(table[:, here].astype(F32), state[:, here], grad)

    def target_copy(c):
        here = aligned(c, CHUNK)
        return send(tgt_ref.at[:, here], tgt_out.at[:, here], t_s.at[c], t_r.at[c], "y", 2)

    def target_step(c, _):
        here, (new, new_state) = rows_step(c, tgt_ref, tgt_state, gt_hi, gt_lo, oh_d, q_low, w_t)
        tgt_ref[:, here] = new.astype(BF16)
        tgt_state[:, here] = new_state
        return 0

    def source_copy(c):
        here = aligned(c, CHUNK)
        return pltpu.make_async_copy(src_ref.at[:, here], src_out.at[:, here], so_sem.at[c])

    def source_step(c, _):
        here, (new, new_state) = rows_step(c, src_ref, src_state, gs_hi, gs_lo, oh_s, p_low, w_s)
        src_ref[:, here] = new.astype(BF16)
        src_state[:, here] = new_state
        source_copy(c).start()
        return 0

    def target_first(c, _):
        target_step(c, 0)
        target_copy(c).start()
        return 0

    lax.fori_loop(0, 2, target_first, 0)
    for i in range(3):
        x_copy(i).wait_recv()
    mine = pl.ds(2 * x, 2)
    at_z[:, :PART] = (
        other[mine].astype(F32) + from_x[0].astype(F32) + from_x[1].astype(F32) + from_x[2].astype(F32)
    ).astype(BF16)
    z_hops, y_hops = HOPS["z"], HOPS["y"]
    z_copies = []
    for i, hop in enumerate(z_hops):
        to = lax.rem(z + hop, 8)
        z_copies.append(send(at_z.at[to // 4, aligned(to % 4, 64)], from_z.at[i], z_s.at[i], z_r.at[i], "z", hop))
        z_copies[-1].start()
    lax.fori_loop(2, 4, target_step, 0)
    for copy in z_copies:
        copy.wait_recv()
    summed = at_z[z // 4, aligned(z % 4, 64), :].astype(F32)
    for i in range(7):
        summed = summed + from_z[i].astype(F32)
    from_y[y] = summed.astype(BF16)
    y_copies = []
    for i, hop in enumerate(y_hops):
        y_copies.append(send(from_y.at[y], from_y.at[y], y_s.at[i], y_r.at[i], "y", hop))
        y_copies[-1].start()
    lax.fori_loop(0, 1, source_step, 0)
    for copy in y_copies:
        copy.wait_recv()
    summed = from_y[0].astype(F32) + from_y[1].astype(F32) + from_y[2].astype(F32) + from_y[3].astype(F32)
    got_y[...] = summed.astype(BF16)
    slot = got.at[core, x, z // 4, aligned(z % 4, 64)]

    def z_back(hop):
        return send(got_y, slot, gz_s.at[hop], gz_r.at[hop], "z", hop)

    for hop in z_hops:
        z_back(hop).start()
    got[core, x, z // 4, aligned(z % 4, 64), :] = got_y[...]
    target_copy(2).start()
    target_copy(3).start()
    state_copy = send(tgt_state, tgt_state_out, ts_s, ts_r, "y", 2)
    state_copy.start()
    lax.fori_loop(1, 3, source_step, 0)

    lane_tile = (z // 4, 1 - z // 4)

    def tile_copy(k, index, send_sem, recv_sem, axis, hop):
        ready = got.at[core, index, lane_tile[k], pl.ds(0, PART)]
        return send(ready, ready, send_sem, recv_sem, axis, hop)

    arrival = (x,) + tuple(lax.rem(x + 4 - hop, 4) for hop in HOPS["x"])

    def x_back(k, i):
        return tile_copy(k, x, gx_s.at[3 * k + i], gx_r.at[3 * k + i], "x", HOPS["x"][i])

    def core_back(k, i):
        return tile_copy(k, arrival[i], gc_s.at[4 * k + i], gc_r.at[4 * k + i], "core", 1)

    for k in range(2):
        for step in range(1 - k, 4):
            owner = lane_tile[k] * 4 + (z + step) % 4
            hop = lax.rem(z - owner + 8, 8)
            pltpu.make_async_remote_copy(
                src_ref=got_y, dst_ref=got.at[core, x, owner // 4, aligned(owner % 4, 64)],
                send_sem=gz_s.at[hop], recv_sem=gz_r.at[hop],
                device_id=peer(me, "z", hop), device_id_type=MESH,
            ).wait_recv()
        for i in range(3):
            x_back(k, i).start()
        core_back(k, 0).start()
    lax.fori_loop(3, 4, source_step, 0)

    source_state_copy = pltpu.make_async_copy(src_state, src_state_out, state_sem.at[0])
    source_state_copy.start()

    def relation_copy(k, i):
        here = aligned(2 * arrival[i] + lane_tile[k], 128)
        return pltpu.make_async_copy(rel_ref.at[:, here], rel_out.at[:, here], ro_sem.at[4 * k + i])

    def relation_rows(k, i):
        core_back(k, i).wait_recv()
        j, t = arrival[i], lane_tile[k]
        here = aligned(2 * j + t, 128)
        grad = jnp.concatenate([got[0, j, t, :PART], got[1, j, t, : W - PART]], axis=0).astype(F32)
        new, new_state = update(rel_ref[:, here], rel_state[:, here], grad)
        rel_ref[:, here] = new
        rel_state[:, here] = new_state
        relation_copy(k, i).start()

    relation_rows(0, 0)
    waiting = (1, 0)
    for k in range(2):
        for i in range(3):
            x_back(k, i).wait_recv()
            core_back(k, i + 1).start()
            relation_rows(*waiting)
            waiting = (k, i + 1)
    relation_rows(*waiting)
    relation_state_copy = pltpu.make_async_copy(rel_state, rel_state_out, state_sem.at[1])
    relation_state_copy.start()
    source_state_copy.wait()
    for i in range(4):
        source_copy(i).wait()
        core_copy(i).wait_send()
        target_copy(i).wait()
    for i in range(3):
        x_copy(i).wait_send()
    for copy in z_copies + y_copies:
        copy.wait_send()
    for hop in z_hops:
        z_back(hop).wait_send()
    for k in range(2):
        for i in range(3):
            x_back(k, i).wait_send()
        for i in range(4):
            core_back(k, i).wait_send()
    state_copy.wait()
    for k in range(2):
        for i in range(4):
            relation_copy(k, i).wait()
    relation_state_copy.wait()


def finish_kernel(*refs):
    ins, outs, stages, in_sem, out_sem = refs[:6], refs[6:12], refs[12:18], refs[18], refs[19]
    loads, stores = [], []
    for part in range(2):
        for i, (here, stage, there) in enumerate(zip(ins, stages, outs)):
            if here.shape[0] == 1:
                if part:
                    continue
                rows = pl.ds(0, 1)
            else:
                rows = pl.ds(part * 208, 192 if part else 208)
            loads.append(pltpu.make_async_copy(here.at[rows], stage.at[rows], in_sem.at[part, i]))
            stores.append(pltpu.make_async_copy(stage.at[rows], there.at[rows], out_sem.at[part, i]))
    for load in loads:
        load.start()
    for load, store in zip(loads, stores):
        load.wait()
        store.start()
    for store in stores:
        store.wait()


def shards(src, src_state, tgt, tgt_state, rel, rel_state, sid, rid, did, sneg, tneg, live):
    sm = pl.BlockSpec(memory_space=pltpu.SMEM)
    hbm = pl.BlockSpec(memory_space=pltpu.HBM)
    shape = jax.ShapeDtypeStruct
    dma = pltpu.SemaphoreType.DMA

    def vmem(*dims, dtype=BF16):
        return pltpu.VMEM(dims, dtype)

    def like(ref):
        return pltpu.VMEM(ref.shape, ref.dtype)

    rows_bf, row_f = shape((W, ROWS), BF16), shape((1, ROWS), F32)
    rows_f, ids, negs = shape((W, ROWS), F32), shape((1, EDGES), jnp.int32), shape(sneg.shape, jnp.int32)
    wide = [(1, ROWS), (1, EDGES)]
    results = (rows_bf, row_f, rows_bf, row_f, rows_f, row_f)
    outs = pl.pallas_call(
        bucket_kernel,
        out_shape=results,
        in_specs=[sm] + [hbm] * 11,
        out_specs=[hbm] * 6,
        scratch_shapes=[like(r) for r in (*results, ids, ids, ids, negs, negs)]
        + [dma((11,)), vmem(ROWS, W), vmem(ROWS, W), vmem(2 * (W - LANE_ROWS), ROWS)]
        + [vmem(ROWS, EDGES)] * 5
        + [vmem(W, EDGES)] * 7
        + [
            vmem(8, 2 * PART, 128), vmem(8, PART, 128),
            vmem(3, 2, PART, 128), vmem(2, 256, 128), vmem(7, 64, 128), vmem(4, 64, 128), vmem(64, 128),
            vmem(2, 4, 2, 256, 128),
        ]
        + [dma((n,)) for n in (4, 4, 3, 3, 7, 7, 3, 3, 8, 8, 6, 6, 8, 8, 4, 4, 4, 8)]
        + [dma(()), dma(()), dma((2,))],
        compiler_params=pltpu.CompilerParams(
            collective_id=0, has_side_effects=True, vmem_limit_bytes=60 * 2**20
        ),
        name="bucket",
    )(live, src.T, src_state.reshape(wide[0]), tgt.T, tgt_state.reshape(wide[0]), rel.T, rel_state.reshape(wide[0]),
      sid.reshape(wide[1]), rid.reshape(wide[1]), did.reshape(wide[1]), sneg, tneg)
    outs = pl.pallas_call(
        finish_kernel,
        out_shape=results,
        in_specs=[hbm] * 6,
        out_specs=[hbm] * 6,
        scratch_shapes=[like(r) for r in results] + [dma((2, 6)), dma((2, 6))],
        compiler_params=pltpu.CompilerParams(vmem_limit_bytes=60 * 2**20),
        name="finish",
    )(*outs)
    return (outs[0].T, outs[1].reshape(ROWS), outs[2].T, outs[3].reshape(ROWS), outs[4].T, outs[5].reshape(ROWS))


def solution(mesh):
    split_rows, split_one, copied = P(("blk", "grp"), None), P(("blk", "grp")), P()
    return jax.shard_map(
        shards,
        mesh=mesh,
        in_specs=(split_rows, split_one, split_rows, split_one, copied, copied,
                  split_one, split_one, split_one, split_rows, split_rows, split_one),
        out_specs=(split_rows, split_one, split_rows, split_one, copied, copied),
        check_vma=False,
    )
```

```python
import jax
import jax.numpy as jnp
from jax import lax
from jax.experimental import pallas as pl
from jax.experimental.pallas import tpu as pltpu
from jax.sharding import PartitionSpec as P

F32, BF16 = jnp.float32, jnp.bfloat16
W, HALF, ROWS, EDGES, BLOCK, NEG = 400, 200, 1024, 2048, 128, 1024
CHUNK = 256
EDGE_CHUNK = 1024
LANE_ROWS = 320
PART = 208
RATE = 0.1
NN = (((1,), (0,)), ((), ()))
NT = (((1,), (1,)), ((), ()))
MESH = pl.DeviceIdType.MESH
SIZE = {"y": 4, "x": 4, "z": 8, "core": 2}
HOPS = {"y": (2, 1, 3), "x": (2, 1, 3), "z": (4, 3, 5, 2, 6, 1, 7), "core": (1,)}


def place():
    blk, grp = lax.axis_index("blk"), lax.axis_index("grp")
    return {"y": blk // 16, "x": blk // 4 % 4, "z": grp * 2 + blk // 2 % 2, "core": blk % 2}


def peer(me, axis, hop):
    at = dict(me)
    at[axis] = lax.rem(me[axis] + hop, SIZE[axis])
    return (at["y"] * 16 + at["x"] * 4 + at["z"] % 2 * 2 + at["core"], at["z"] // 2)


def dot(a, b, dims=NN):
    return lax.dot_general(a, b, dims, preferred_element_type=F32)


def mul(a, b):
    ar, ai, br, bi = a[:HALF], a[HALF:], b[:HALF], b[HALF:]
    return jnp.concatenate([ar * br - ai * bi, ar * bi + ai * br], axis=0)


def mulc(a, b):
    ar, ai, br, bi = a[:HALF], a[HALF:], b[:HALF], b[HALF:]
    return jnp.concatenate([ar * br + ai * bi, ai * br - ar * bi], axis=0)


def split(x):
    hi = x.astype(BF16)
    return hi, (x - hi.astype(F32)).astype(BF16)


def one_hot(ids, count):
    at = lax.broadcasted_iota(jnp.int32, (count, ids.shape[1]), 0)
    return jnp.where(at == ids, 1.0, 0.0).astype(BF16)


def pick(table, ids, rows):
    low, high = ids % 128, ids // 128
    parts = []
    for b in range(ids.shape[1] // 128):
        lanes = slice(128 * b, 128 * b + 128)
        at = jnp.broadcast_to(low[:, lanes], (rows, 128))
        tile = jnp.broadcast_to(high[:, lanes], (rows, 128))
        out = jnp.take_along_axis(table[:rows, :128], at, axis=1, mode="promise_in_bounds")
        for t in range(1, ROWS // 128):
            got = jnp.take_along_axis(table[:rows, 128 * t : 128 * t + 128], at, axis=1, mode="promise_in_bounds")
            out = jnp.where(tile == t, got, out)
        parts.append(out)
    return jnp.concatenate(parts, axis=1)


def counts_of(ids, scale):
    grid = dot(one_hot(ids % 32, 32), one_hot(ids // 32, 32), NT) * scale
    return jnp.concatenate([jnp.broadcast_to(grid[:, h : h + 1], (32, BLOCK)) for h in range(32)], axis=0)


def weights_of(scores, count):
    return (count + count * jnp.tanh(scores)).astype(BF16)


def update(table, state, grad):
    new_state = state + jnp.sum(grad * grad, axis=0, keepdims=True) * (1.0 / W)
    return table - RATE * grad * lax.rsqrt(new_state), new_state


def aligned(index, size):
    return pl.ds(pl.multiple_of(index * size, size), size)


def bucket_kernel(
    live_ref, src_h, src_state_h, tgt_h, tgt_state_h, rel_h, rel_state_h, sid_h, rid_h, did_h, sneg_h, tneg_h,
    src_out, src_state_out, tgt_out, tgt_state_out, rel_out, rel_state_out,
    src_ref, src_state, tgt_ref, tgt_state, rel_ref, rel_state, sid_ref, rid_ref, did_ref, sneg_ref, tneg_ref, in_sem,
    src_t, tgt_t, rel_hl, oh_s, oh_d, oh_r, w_s, w_t, q_low, p_low, gs_hi, gs_lo, gt_hi, gt_lo, rt,
    own, other, from_x, at_z, from_z, from_y, got_y, got,
    core_s, core_r, x_s, x_r, z_s, z_r, y_s, y_r, gz_s, gz_r, gx_s, gx_r, gc_s, gc_r,
    t_s, t_r, so_sem, ro_sem, ts_s, ts_r, state_sem,
):
    loads = [
        pltpu.make_async_copy(here, there, in_sem.at[i])
        for i, (here, there) in enumerate([
            (src_h, src_ref), (tgt_h, tgt_ref), (rel_h, rel_ref), (sid_h, sid_ref), (rid_h, rid_ref), (did_h, did_ref),
            (sneg_h, sneg_ref), (tneg_h, tneg_ref), (src_state_h, src_state), (tgt_state_h, tgt_state),
            (rel_state_h, rel_state),
        ])
    ]
    for load in loads:
        load.start()
    me = place()
    core, x, y, z = me["core"], me["x"], me["y"], me["z"]
    barrier = pltpu.get_barrier_semaphore()
    total = 0
    for axis, hops in HOPS.items():
        for hop in hops:
            pl.semaphore_signal(barrier, inc=1, device_id=peer(me, axis, hop), device_id_type=MESH)
            total += 1

    def send(src, dst, send_sem, recv_sem, axis, hop):
        return pltpu.make_async_remote_copy(
            src_ref=src, dst_ref=dst, send_sem=send_sem, recv_sem=recv_sem,
            device_id=peer(me, axis, hop), device_id_type=MESH,
        )

    own[:, W:] = jnp.zeros((8, 2 * PART - W, 128), BF16)
    at_z[:, PART:] = jnp.zeros((2, 256 - PART, 128), BF16)
    loads[0].wait()
    src_t[...] = (0.5 * src_ref[...].astype(F32)).T.astype(BF16)
    loads[1].wait()
    tgt_t[...] = (0.5 * tgt_ref[...].astype(F32)).T.astype(BF16)
    for load in loads[2:]:
        load.wait()
    rel_hl[: W - LANE_ROWS], rel_hl[W - LANE_ROWS :] = split(rel_ref[LANE_ROWS:])
    count = live_ref[0]

    def edges(c, _):
        first = pl.multiple_of(c * EDGE_CHUNK, EDGE_CHUNK)
        here = pl.ds(first, EDGE_CHUNK)
        slots = first + lax.broadcasted_iota(jnp.int32, (1, EDGE_CHUNK), 1)
        alive = jnp.where(slots < count, 1.0, 0.0).astype(F32)

        def block_counts(negs):
            blocks = []
            for i in range(EDGE_CHUNK // BLOCK):
                scale = jnp.where(first + i * BLOCK < count, 0.5 / NEG, 0.0).astype(F32)
                blocks.append(counts_of(negs[pl.ds(c * (EDGE_CHUNK // BLOCK) + i, 1), :], scale))
            return jnp.concatenate(blocks, axis=1)

        ohs = one_hot(sid_ref[:, here], ROWS)
        ohd = one_hot(did_ref[:, here], ROWS)
        ohr = one_hot(rid_ref[:, here], ROWS)
        oh_s[:, here] = ohs
        oh_d[:, here] = ohd
        oh_r[:, here] = ohr
        s = dot(src_ref[...], ohs)
        d = dot(tgt_ref[...], ohd)
        low = dot(rel_hl[...], ohr)
        r = jnp.concatenate(
            [pick(rel_ref, rid_ref[:, here], LANE_ROWS), low[: W - LANE_ROWS] + low[W - LANE_ROWS :]], axis=0
        )
        q = mul(s, r)
        p = mulc(r, d)
        pos = jnp.sum(q * d, axis=0, keepdims=True)
        pos_grad = -alive / (1.0 + jnp.exp(pos))
        ql = q.astype(BF16)
        plow = p.astype(BF16)
        q_low[:, here] = ql
        p_low[:, here] = plow
        wt = weights_of(dot(tgt_t[...], ql), block_counts(tneg_ref))
        w_t[:, here] = wt
        ws = weights_of(dot(src_t[...], plow), block_counts(sneg_ref))
        w_s[:, here] = ws
        qg = pos_grad * d + dot(tgt_ref[...], wt)
        pg = dot(src_ref[...], ws)
        gs_hi[:, here], gs_lo[:, here] = split(mulc(qg, r))
        gt_hi[:, here], gt_lo[:, here] = split(pos_grad * q + mul(pg, r))
        rt[:, here] = (mulc(qg, s) + mulc(d, pg)).astype(BF16)
        return 0

    lax.fori_loop(0, EDGES // EDGE_CHUNK, edges, 0)
    pl.semaphore_wait(barrier, total)

    half = aligned(core, PART)
    far = aligned(1 - core, PART)
    order = HOPS["x"] + (0,)

    def piece(i):
        return lax.rem(x + order[i], 4)

    def core_copy(i):
        tiles = pl.ds(2 * piece(i), 2)
        return send(own.at[tiles, far], other.at[tiles], core_s.at[i], core_r.at[i], "core", 1)

    tile_out = (1 - z // 4, z // 4)

    def x_copy(i, k):
        return send(
            other.at[2 * piece(i) + tile_out[k]], from_x.at[i, tile_out[k]],
            x_s.at[2 * i + k], x_r.at[2 * i + k], "x", order[i],
        )

    def relation_piece(i):
        j = piece(i)
        grad = dot(rt[...], oh_r[aligned(j, CHUNK), :], NT).astype(BF16)
        own[2 * j, :W] = grad[:, :128]
        own[2 * j + 1, :W] = grad[:, 128:]
        core_copy(i).start()

    def core_add(i):
        core_copy(i).wait_recv()
        tiles = pl.ds(2 * piece(i), 2)
        other[tiles] = (other[tiles].astype(F32) + own[tiles, half].astype(F32)).astype(BF16)

    for i in range(4):
        relation_piece(i)
        if i:
            core_add(i - 1)
            x_copy(i - 1, 0).start()
            x_copy(i - 1, 1).start()
    core_add(3)

    def rows_step(c, table, state, hi_ref, lo_ref, oh, low, wts):
        here = aligned(c, CHUNK)
        grad = dot(hi_ref[...], oh[here, :], NT) + dot(lo_ref[...], oh[here, :], NT) + dot(low[...], wts[here, :], NT)
        return here, update(table[:, here].astype(F32), state[:, here], grad)

    def target_copy(c):
        here = aligned(c, CHUNK)
        return send(tgt_ref.at[:, here], tgt_out.at[:, here], t_s.at[c], t_r.at[c], "y", 2)

    def target_step(c, _):
        here, (new, new_state) = rows_step(c, tgt_ref, tgt_state, gt_hi, gt_lo, oh_d, q_low, w_t)
        tgt_ref[:, here] = new.astype(BF16)
        tgt_state[:, here] = new_state
        return 0

    def source_copy(c):
        here = aligned(c, CHUNK)
        return pltpu.make_async_copy(src_ref.at[:, here], src_out.at[:, here], so_sem.at[c])

    def source_step(c, _):
        here, (new, new_state) = rows_step(c, src_ref, src_state, gs_hi, gs_lo, oh_s, p_low, w_s)
        src_ref[:, here] = new.astype(BF16)
        src_state[:, here] = new_state
        source_copy(c).start()
        return 0

    def target_first(c, _):
        target_step(c, 0)
        target_copy(c).start()
        return 0

    lax.fori_loop(0, 2, target_first, 0)
    z_hops, y_hops = HOPS["z"], HOPS["y"]

    def z_copy(tile, owner, hop):
        return send(at_z.at[tile, aligned(owner % 4, 64)], from_z.at[hop], z_s.at[hop], z_r.at[hop], "z", hop)

    for k in range(2):
        for i in range(3):
            x_copy(i, k).wait_recv()
        t = tile_out[k]
        at_z[t, :PART] = (
            other[2 * x + t].astype(F32) + from_x[0, t].astype(F32) + from_x[1, t].astype(F32) + from_x[2, t].astype(F32)
        ).astype(BF16)
        for step in range(k, 4):
            owner = t * 4 + (z + step) % 4
            z_copy(t, owner, lax.rem(owner - z + 8, 8)).start()
    lax.fori_loop(2, 4, target_step, 0)
    for hop in range(1, 8):
        z_copy(0, 0, hop).wait_recv()
    summed = at_z[z // 4, aligned(z % 4, 64), :].astype(F32)
    for hop in range(1, 8):
        summed = summed + from_z[hop].astype(F32)
    from_y[y] = summed.astype(BF16)
    y_copies = []
    for i, hop in enumerate(y_hops):
        y_copies.append(send(from_y.at[y], from_y.at[y], y_s.at[i], y_r.at[i], "y", hop))
        y_copies[-1].start()
    lax.fori_loop(0, 1, source_step, 0)
    for copy in y_copies:
        copy.wait_recv()
    summed = from_y[0].astype(F32) + from_y[1].astype(F32) + from_y[2].astype(F32) + from_y[3].astype(F32)
    got_y[...] = summed.astype(BF16)
    slot = got.at[core, x, z // 4, aligned(z % 4, 64)]

    def z_back(hop):
        return send(got_y, slot, gz_s.at[hop], gz_r.at[hop], "z", hop)

    for hop in z_hops:
        z_back(hop).start()
    got[core, x, z // 4, aligned(z % 4, 64), :] = got_y[...]
    target_copy(2).start()
    target_copy(3).start()
    state_copy = send(tgt_state, tgt_state_out, ts_s, ts_r, "y", 2)
    state_copy.start()
    lax.fori_loop(1, 3, source_step, 0)

    lane_tile = (z // 4, 1 - z // 4)

    def tile_copy(k, index, send_sem, recv_sem, axis, hop):
        ready = got.at[core, index, lane_tile[k], pl.ds(0, PART)]
        return send(ready, ready, send_sem, recv_sem, axis, hop)

    arrival = (x,) + tuple(lax.rem(x + 4 - hop, 4) for hop in HOPS["x"])

    def x_back(k, i):
        return tile_copy(k, x, gx_s.at[3 * k + i], gx_r.at[3 * k + i], "x", HOPS["x"][i])

    def core_back(k, i):
        return tile_copy(k, arrival[i], gc_s.at[4 * k + i], gc_r.at[4 * k + i], "core", 1)

    for k in range(2):
        for step in range(1 - k, 4):
            owner = lane_tile[k] * 4 + (z + step) % 4
            hop = lax.rem(z - owner + 8, 8)
            pltpu.make_async_remote_copy(
                src_ref=got_y, dst_ref=got.at[core, x, owner // 4, aligned(owner % 4, 64)],
                send_sem=gz_s.at[hop], recv_sem=gz_r.at[hop],
                device_id=peer(me, "z", hop), device_id_type=MESH,
            ).wait_recv()
        for i in range(3):
            x_back(k, i).start()
        core_back(k, 0).start()
    lax.fori_loop(3, 4, source_step, 0)

    source_state_copy = pltpu.make_async_copy(src_state, src_state_out, state_sem.at[0])
    source_state_copy.start()

    def relation_copy(k, i):
        here = aligned(2 * arrival[i] + lane_tile[k], 128)
        return pltpu.make_async_copy(rel_ref.at[:, here], rel_out.at[:, here], ro_sem.at[4 * k + i])

    def relation_rows(k, i):
        core_back(k, i).wait_recv()
        j, t = arrival[i], lane_tile[k]
        here = aligned(2 * j + t, 128)
        grad = jnp.concatenate([got[0, j, t, :PART], got[1, j, t, : W - PART]], axis=0).astype(F32)
        new, new_state = update(rel_ref[:, here], rel_state[:, here], grad)
        rel_ref[:, here] = new
        rel_state[:, here] = new_state
        relation_copy(k, i).start()

    relation_rows(0, 0)
    waiting = (1, 0)
    for k in range(2):
        for i in range(3):
            x_back(k, i).wait_recv()
            core_back(k, i + 1).start()
            relation_rows(*waiting)
            waiting = (k, i + 1)
    relation_rows(*waiting)
    relation_state_copy = pltpu.make_async_copy(rel_state, rel_state_out, state_sem.at[1])
    relation_state_copy.start()
    source_state_copy.wait()
    for i in range(4):
        source_copy(i).wait()
        core_copy(i).wait_send()
        target_copy(i).wait()
    for i in range(3):
        for k in range(2):
            x_copy(i, k).wait_send()
    for copy in y_copies:
        copy.wait_send()
    for hop in range(1, 8):
        z_copy(0, 0, hop).wait_send()
    for hop in z_hops:
        z_back(hop).wait_send()
    for k in range(2):
        for i in range(3):
            x_back(k, i).wait_send()
        for i in range(4):
            core_back(k, i).wait_send()
    state_copy.wait()
    for k in range(2):
        for i in range(4):
            relation_copy(k, i).wait()
    relation_state_copy.wait()


def finish_kernel(*refs):
    ins, outs, stages, in_sem, out_sem = refs[:6], refs[6:12], refs[12:18], refs[18], refs[19]
    loads, stores = [], []
    for part in range(2):
        for i, (here, stage, there) in enumerate(zip(ins, stages, outs)):
            if here.shape[0] == 1:
                if part:
                    continue
                rows = pl.ds(0, 1)
            else:
                rows = pl.ds(part * 208, 192 if part else 208)
            loads.append(pltpu.make_async_copy(here.at[rows], stage.at[rows], in_sem.at[part, i]))
            stores.append(pltpu.make_async_copy(stage.at[rows], there.at[rows], out_sem.at[part, i]))
    for load in loads:
        load.start()
    for load, store in zip(loads, stores):
        load.wait()
        store.start()
    for store in stores:
        store.wait()


def shards(src, src_state, tgt, tgt_state, rel, rel_state, sid, rid, did, sneg, tneg, live):
    sm = pl.BlockSpec(memory_space=pltpu.SMEM)
    hbm = pl.BlockSpec(memory_space=pltpu.HBM)
    shape = jax.ShapeDtypeStruct
    dma = pltpu.SemaphoreType.DMA

    def vmem(*dims, dtype=BF16):
        return pltpu.VMEM(dims, dtype)

    def like(ref):
        return pltpu.VMEM(ref.shape, ref.dtype)

    rows_bf, row_f = shape((W, ROWS), BF16), shape((1, ROWS), F32)
    rows_f, ids, negs = shape((W, ROWS), F32), shape((1, EDGES), jnp.int32), shape(sneg.shape, jnp.int32)
    wide = [(1, ROWS), (1, EDGES)]
    results = (rows_bf, row_f, rows_bf, row_f, rows_f, row_f)
    outs = pl.pallas_call(
        bucket_kernel,
        out_shape=results,
        in_specs=[sm] + [hbm] * 11,
        out_specs=[hbm] * 6,
        scratch_shapes=[like(r) for r in (*results, ids, ids, ids, negs, negs)]
        + [dma((11,)), vmem(ROWS, W), vmem(ROWS, W), vmem(2 * (W - LANE_ROWS), ROWS)]
        + [vmem(ROWS, EDGES)] * 5
        + [vmem(W, EDGES)] * 7
        + [
            vmem(8, 2 * PART, 128), vmem(8, PART, 128),
            vmem(3, 2, PART, 128), vmem(2, 256, 128), vmem(8, 64, 128), vmem(4, 64, 128), vmem(64, 128),
            vmem(2, 4, 2, 256, 128),
        ]
        + [dma((n,)) for n in (4, 4, 6, 6, 8, 8, 3, 3, 8, 8, 6, 6, 8, 8, 4, 4, 4, 8)]
        + [dma(()), dma(()), dma((2,))],
        compiler_params=pltpu.CompilerParams(
            collective_id=0, has_side_effects=True, vmem_limit_bytes=60 * 2**20
        ),
        name="bucket",
    )(live, src.T, src_state.reshape(wide[0]), tgt.T, tgt_state.reshape(wide[0]), rel.T, rel_state.reshape(wide[0]),
      sid.reshape(wide[1]), rid.reshape(wide[1]), did.reshape(wide[1]), sneg, tneg)
    outs = pl.pallas_call(
        finish_kernel,
        out_shape=results,
        in_specs=[hbm] * 6,
        out_specs=[hbm] * 6,
        scratch_shapes=[like(r) for r in results] + [dma((2, 6)), dma((2, 6))],
        compiler_params=pltpu.CompilerParams(vmem_limit_bytes=60 * 2**20),
        name="finish",
    )(*outs)
    return (outs[0].T, outs[1].reshape(ROWS), outs[2].T, outs[3].reshape(ROWS), outs[4].T, outs[5].reshape(ROWS))


def solution(mesh):
    split_rows, split_one, copied = P(("blk", "grp"), None), P(("blk", "grp")), P()
    return jax.shard_map(
        shards,
        mesh=mesh,
        in_specs=(split_rows, split_one, split_rows, split_one, copied, copied,
                  split_one, split_one, split_one, split_rows, split_rows, split_one),
        out_specs=(split_rows, split_one, split_rows, split_one, copied, copied),
        check_vma=False,
    )
```
